256 devices in a mesh: blk: 16 (over z, core), mer: 8 (over x, y_lo), ply: 2 (over y_hi).
Axes of the slice: x: 4, y: 4 (y_hi: 2, y_lo: 2; y = y_hi * 2 + y_lo), z: 8, core: 2. Of those that a mesh axis runs over, the one named last changes fastest.
Arguments:
- connectivity: int32 [8, 524288], P(None, ('blk', 'mer', 'ply')), may hold values from 0 to 2943, as said below
- slot_map: int32 [64, 524288], P(None, ('blk', 'mer', 'ply')), may hold values from 0 to 26
- material_ids: int32 [524288], P(('blk', 'mer', 'ply')), may hold values from 0 to 7
- element_counts: int32 [256], P(('blk', 'mer', 'ply')), may hold values from 144 to 1152, as said below
- inverse_jacobians: float32 [72, 524288], P(None, ('blk', 'mer', 'ply')), may hold values from -5 to 5
- quadrature_weights: float32 [8, 524288], P(None, ('blk', 'mer', 'ply')), may hold values from 0.02 to 0.2
- materials: float32 [3, 8], replicated, may hold values from 0.3 to 3
- displacement: float32 [3, 524288], P(None, ('blk', 'mer', 'ply')), may hold values from -1.8 to 1.8
- previous: float32 [3, 524288], P(None, ('blk', 'mer', 'ply')), may hold values from -1.8 to 1.8
- load: float32 [3, 524288], P(None, ('blk', 'mer', 'ply')), may hold values from -6 to 6
Outputs:
- residual: float32 [3, 524288], P(None, ('blk', 'mer', 'ply'))
- tangent: float32 [243, 524288], P(None, ('blk', 'mer', 'ply'))
The draws below stay inside these ranges and needn't reach their ends.
Inputs may be any that keep to these rules, and one draw needn't show every extreme that they name: `connectivity`: column e is an element slot; device d holds columns 2048 * d to 2048 * d + 2047 and owns nodes 2048 * d to 2048 * d + 2047. Rows 0 to 3 are below 2048, and so are rows 4 to 7 except: in the last 512 columns of a device they lie in 2048 to 2559; in the 256 columns before those, where the device has a mer index + 1, in 2560 to 2815; in the 128 columns before those, where the device has a ply index + 1, in the rows above that. `slot_map`: entry [8 a + b, e] is the slot, within the block row of corner a, that receives the block of the corner pair (a, b). `material_ids`: columns of materials. `element_counts`: interior slots (slot number below 1152 within the device) at or above the count are padding.
All inputs are finite; a program needn't handle non-finite values.
Results may differ from the reference program's by a relative error of at most 0.00028.
Values sent between devices are 32-bit elements; how exact they have to be, the bound alone decides.
No kernel may reach another device: no remote copies, remote signals or barrier semaphores. Data moves between devices by JAX's collectives and lax.ppermute only.
A program may use at most 256 MiB of HBM per device.

```python
import math
import jax
import jax.numpy as jnp
from jax import lax

NODE_DEV = 2048
SLOTS = 27
MATS = 8
ELEM_DEV = 2048
FACE_BLK = 512
FACE_MER = 256
FACE_PLY = 128
INNER = 1152
CYCLE = 16
MERS = 8
PLIES = 2
NODES = 524288
ELEMS = 524288
DEVICES = 256


def draw_connectivity(key, part):
    key = jax.random.fold_in(key, 7)
    keys = jax.random.split(key, 4)
    slot_index = jnp.arange(ELEMS, dtype=jnp.int32)
    device = slot_index // ELEM_DEV
    local = slot_index % ELEM_DEV
    mer_pos = device // PLIES % MERS
    ply_pos = device % PLIES
    own = jax.random.randint(keys[0], (8, ELEMS), 0, NODE_DEV, dtype=jnp.int32)
    row_sel = jnp.arange(8, dtype=jnp.int32)[:, None]
    own = jnp.where((row_sel == 0) & (local == 0), NODE_DEV - 1, own)
    own = jnp.where((row_sel == 1) & (local == 0), 0, own)
    face_b = jax.random.randint(keys[1], (4, ELEMS), 0, FACE_BLK, dtype=jnp.int32)
    face_m = jax.random.randint(keys[2], (4, ELEMS), 0, FACE_MER, dtype=jnp.int32)
    face_p = jax.random.randint(keys[3], (4, ELEMS), 0, FACE_PLY, dtype=jnp.int32)
    upper_sel = jnp.arange(4, dtype=jnp.int32)[:, None]
    face_b = jnp.where((upper_sel == 0) & (local == ELEM_DEV - 1), FACE_BLK - 1, face_b)
    face_m = jnp.where((upper_sel == 0) & (local == ELEM_DEV - FACE_BLK - 1), FACE_MER - 1, face_m)
    face_p = jnp.where((upper_sel == 0) & (local == INNER + FACE_PLY - 1), FACE_PLY - 1, face_p)
    seg_blk = local >= ELEM_DEV - FACE_BLK
    seg_mer = (local >= INNER + FACE_PLY) & (local < ELEM_DEV - FACE_BLK) & (mer_pos < MERS - 1)
    seg_ply = (local >= INNER) & (local < INNER + FACE_PLY) & (ply_pos < PLIES - 1)
    upper = jnp.where(seg_blk, NODE_DEV + face_b, jnp.where(seg_mer, NODE_DEV + FACE_BLK + face_m, jnp.where(seg_ply, NODE_DEV + FACE_BLK + FACE_MER + face_p, own[4:8])))
    return jnp.concatenate([own[0:4], upper], axis=0).astype(jnp.int32)


def draw_element_counts(key, part):
    key = jax.random.fold_in(key, 11)
    keys = jax.random.split(key, 2)
    device = jnp.arange(DEVICES, dtype=jnp.int32)
    cycle_pos = device // (MERS * PLIES)
    patch = jax.random.randint(keys[0], (), 0, CYCLE, dtype=jnp.int32)
    nearby = (cycle_pos == patch) | (cycle_pos == (patch + 1) % CYCLE)
    light = jax.random.randint(keys[1], (DEVICES,), INNER // 8, INNER // 4 + 1, dtype=jnp.int32)
    return jnp.where(nearby, INNER, light).astype(jnp.int32)


def place_ends(result, stream_key, low, top_value):
    extent = result.shape
    spot = [jax.random.randint(jax.random.fold_in(stream_key, axis), (), 0, extent[axis]) for axis in range(len(extent))]
    result = result.at[tuple(spot)].set(low)
    longest = extent.index(max(extent))
    spot[longest] = (spot[longest] + 1) % extent[longest]
    return result.at[tuple(spot)].set(top_value)


def block_scale(key, extent, cuts, low, top_value):
    def one(axis_at, parts):
        draws = jax.random.uniform(jax.random.fold_in(jax.random.fold_in(key, 6), axis_at), (parts,), jnp.float32, low / len(cuts), top_value / len(cuts))
        return jnp.repeat(jnp.exp(draws), extent[axis_at] // parts).reshape((-1,) + (1,) * (len(extent) - axis_at - 1))

    factor_of = one(*cuts[0])
    for cut in cuts[1:]:
        factor_of = factor_of * one(*cut)
    return factor_of


def scatter_about(own_key, shape, deviation, limit, cuts=(), kind=jnp.bfloat16):
    factor_of = block_scale(own_key, shape, cuts, -0.22, 0.18) if cuts else 1.0
    values = jax.random.normal(own_key, shape, jnp.float32) * deviation * factor_of
    return jnp.minimum(jnp.maximum(values, -limit), limit).astype(kind)


def setup_inputs(seed: int = 0) -> dict:
    key_of = jax.random.split(jax.random.key(seed), 11)
    return {
        "connectivity": draw_connectivity(jax.random.fold_in(key_of[10], 71), 0),
        "slot_map": place_ends(jax.random.randint(key_of[1], (64, ELEMS), 0, SLOTS), jax.random.fold_in(key_of[1], 1), 0, SLOTS - 1).astype(jnp.int32),
        "material_ids": place_ends(jax.random.randint(key_of[2], (ELEMS,), 0, MATS), jax.random.fold_in(key_of[2], 1), 0, MATS - 1).astype(jnp.int32),
        "element_counts": draw_element_counts(jax.random.fold_in(key_of[10], 71), 0),
        "inverse_jacobians": scatter_about(key_of[4], (72, ELEMS), 1.0, 5.0, ((1, 256),), jnp.float32),
        "quadrature_weights": jnp.clip(jnp.exp(math.log(0.2) - 2.3025851 * jax.random.uniform(key_of[5], (8, ELEMS), jnp.float32) ** block_scale(key_of[5], (8, ELEMS), ((1, 256),), -0.2, 0.2)), 0.02, 0.2),
        "materials": jnp.clip(jnp.exp(jax.random.uniform(key_of[6], (3, MATS), jnp.float32, math.log(0.3), math.log(3.0))), 0.3, 3.0),
        "displacement": scatter_about(key_of[7], (3, NODES), 0.3, 1.8, ((1, 256),), jnp.float32),
        "previous": scatter_about(key_of[8], (3, NODES), 0.3, 1.8, ((1, 256),), jnp.float32),
        "load": scatter_about(key_of[9], (3, NODES), 1.0, 6.0, ((1, 256),), jnp.float32),
    }


HIGH = lax.Precision.HIGHEST

def shape_table():
    signs = [[-1, -1, -1], [1, -1, -1], [1, 1, -1], [-1, 1, -1], [-1, -1, 1], [1, -1, 1], [1, 1, 1], [-1, 1, 1]]
    root = math.sqrt(3.0)
    table = []
    for quad_point in range(8):
        point_rows = []
        for corner_node in range(8):
            entries = []
            for deriv_axis in range(3):
                value = signs[corner_node][deriv_axis] / 8.0
                for other_axis in range(3):
                    if other_axis != deriv_axis:
                        value = value * (1.0 + signs[corner_node][other_axis] * signs[quad_point][other_axis] / root)
                entries.append(value)
            point_rows.append(entries)
        table.append(point_rows)
    return table

def element_terms(inverse_jac, weights, params, nodal):
    width = inverse_jac.shape[1]
    table = jnp.asarray(shape_table(), dtype=jnp.float32)
    inverse = inverse_jac.reshape(8, 3, 3, width)
    grads = jnp.einsum('qak,qkln->qaln', table, inverse, precision=HIGH)
    ident = jnp.eye(3, dtype=jnp.float32)[None, :, :, None]
    deform = ident + jnp.einsum('ian,qaln->qiln', nodal[0:3], grads, precision=HIGH)
    deform_old = ident + jnp.einsum('ian,qaln->qiln', nodal[3:6], grads, precision=HIGH)
    strain = 0.5 * (jnp.einsum('qiln,qimn->qlmn', deform, deform, precision=HIGH) - ident)
    strain_old = 0.5 * (jnp.einsum('qiln,qimn->qlmn', deform_old, deform_old, precision=HIGH) - ident)
    lame = params[0]
    shear = params[1]
    viscous = params[2]
    trace_e = strain[:, 0, 0] + strain[:, 1, 1] + strain[:, 2, 2]
    stress = lame * trace_e[:, None, None, :] * ident + 2.0 * shear * strain + 2.0 * viscous * (strain - strain_old)
    first_pk = jnp.einsum('qimn,qmln->qiln', deform, stress, precision=HIGH)
    element_res = jnp.einsum('qn,qiln,qaln->ain', weights, first_pk, grads, precision=HIGH)
    pushed = jnp.einsum('qiln,qaln->qain', deform, grads, precision=HIGH)
    stress_g = jnp.einsum('qlmn,qbmn->qbln', stress, grads, precision=HIGH)
    geometric = jnp.einsum('qn,qaln,qbln->abn', weights, grads, stress_g, precision=HIGH)
    outer = jnp.einsum('qn,qain,qbjn->abijn', weights, pushed, pushed, precision=HIGH)
    metric = jnp.einsum('qn,qaln,qbln->qabn', weights, grads, grads, precision=HIGH)
    left_cg = jnp.einsum('qimn,qjmn->qijn', deform, deform, precision=HIGH)
    spatial = jnp.einsum('qabn,qijn->abijn', metric, left_cg, precision=HIGH)
    modulus = shear + viscous
    eye_five = jnp.eye(3, dtype=jnp.float32)[None, None, :, :, None]
    element_tan = geometric[:, :, None, None, :] * eye_five + lame * outer + modulus * outer.transpose(1, 0, 2, 3, 4) + modulus * spatial
    return (element_res, element_tan)

def add_terms(accs, element_res, element_tan, rows, slots, living, width_total):
    acc_res, acc_tan = accs
    count_rows = rows.shape[0]
    width = rows.shape[1]
    res_vals = (element_res * living).transpose(1, 0, 2).reshape(3, count_rows * width)
    acc_res = acc_res.at[:, rows.reshape(-1)].add(res_vals)
    tan_vals = (element_tan.reshape(count_rows, 8, 9, width) * living).transpose(2, 0, 1, 3).reshape(9, count_rows * 8 * width)
    columns = (slots.reshape(count_rows, 8, width) * width_total + rows[:, None, :]).reshape(-1)
    acc_tan = acc_tan.at[:, columns].add(tan_vals)
    return (acc_res, acc_tan)

def global_nodes(local_rows, device):
    device = jnp.asarray(device).astype(jnp.int32)
    cycle_pos = device // (MERS * PLIES)
    rest = device % (MERS * PLIES)
    next_blk = (cycle_pos + 1) % CYCLE * (MERS * PLIES) + rest
    first_mer = NODE_DEV + FACE_BLK
    first_ply = first_mer + FACE_MER
    own_node = device * NODE_DEV + local_rows
    blk_node = next_blk * NODE_DEV + local_rows - NODE_DEV
    mer_node = (device + PLIES) * NODE_DEV + local_rows - first_mer
    ply_node = (device + 1) * NODE_DEV + local_rows - first_ply
    nodes = jnp.where(local_rows < NODE_DEV, own_node, jnp.where(local_rows < first_mer, blk_node, jnp.where(local_rows < first_ply, mer_node, ply_node)))
    return nodes.astype(jnp.int32)

def reference(connectivity, slot_map, material_ids, element_counts, inverse_jacobians, quadrature_weights, materials, displacement, previous, load):
    nodal_state = jnp.concatenate([displacement, previous], axis=0)
    onehot = (material_ids[None, :] == jnp.arange(MATS, dtype=jnp.int32)[:, None]).astype(jnp.float32)
    params = jnp.dot(materials, onehot, precision=HIGH)
    local_index = jnp.arange(ELEM_DEV, dtype=jnp.int32)

    def turn_step(turn, accs):
        first_slot = (turn * ELEM_DEV).astype(jnp.int32)
        local_rows = lax.dynamic_slice_in_dim(connectivity, first_slot, ELEM_DEV, 1)
        rows = global_nodes(local_rows, turn)
        slots = lax.dynamic_slice_in_dim(slot_map, first_slot, ELEM_DEV, 1)
        inverse_jac = lax.dynamic_slice_in_dim(inverse_jacobians, first_slot, ELEM_DEV, 1)
        weights = lax.dynamic_slice_in_dim(quadrature_weights, first_slot, ELEM_DEV, 1)
        piece_params = lax.dynamic_slice_in_dim(params, first_slot, ELEM_DEV, 1)
        living = ((local_index >= INNER) | (local_index < element_counts[turn])).astype(jnp.float32)
        nodal = jnp.take(nodal_state, rows, axis=1)
        element_res, element_tan = element_terms(inverse_jac, weights, piece_params, nodal)
        return add_terms(accs, element_res, element_tan, rows, slots, living, NODES)
    start_accs = (jnp.zeros((3, NODES), jnp.float32), jnp.zeros((9, SLOTS * NODES), jnp.float32))
    acc_res, acc_tan = lax.fori_loop(0, DEVICES, turn_step, start_accs)
    return (acc_res - load, acc_tan.reshape(9 * SLOTS, NODES))
```

```python
import math

import jax
import jax.numpy as jnp
from jax import lax
from jax.experimental import pallas as pl
from jax.experimental.pallas import tpu as pltpu
from jax.sharding import PartitionSpec as P

SLOTS = 27
NODES = 2048
ELEMS = 2048
TILES = 16
WAYS = 8
VROWS = 8 * 9 * 64
VMEM = 56 * 1024 * 1024

SIGNS = [
    [-1, -1, -1],
    [1, -1, -1],
    [1, 1, -1],
    [-1, 1, -1],
    [-1, -1, 1],
    [1, -1, 1],
    [1, 1, 1],
    [-1, 1, 1],
]
OTHERS = [(1, 2), (0, 2), (0, 1)]
SYM = [(0, 0), (0, 1), (0, 2), (1, 1), (1, 2), (2, 2)]


def sym(i, j):
    return SYM.index((min(i, j), max(i, j)))


def shape_factors():
    table = []
    for q in range(8):
        for k in range(3):
            m, n = OTHERS[k]
            for sm in (-1, 1):
                for sn in (-1, 1):
                    fm = 1.0 + sm * SIGNS[q][m] / math.sqrt(3.0)
                    fn = 1.0 + sn * SIGNS[q][n] / math.sqrt(3.0)
                    table.append(fm * fn / 8.0)
    return table


def tile_copies(src, dst, rows, first_tile, count, sem):
    return [
        pltpu.make_async_copy(
            src.at[:, pl.ds((first_tile + t) * 128, 128)], dst.at[pl.ds(t * rows, rows), :], sem.at[t]
        )
        for t in range(count)
    ]


def split_table(table, tparts):
    value = table[...]
    high = value.astype(jnp.bfloat16)
    rest = value - high.astype(jnp.float32)
    mid = rest.astype(jnp.bfloat16)
    low = (rest - mid.astype(jnp.float32)).astype(jnp.bfloat16)
    tparts[:, 0:128] = high
    tparts[:, 128:256] = mid
    tparts[:, 256:384] = low


def gather_nodal(conn, tparts, nodal, blocks):
    lanes = lax.broadcasted_iota(jnp.int32, (128, 128), 0)

    def step(t, carry):
        for pair in range(4):
            rows = []
            hots = []
            for c in range(2):
                row = conn[pl.ds(t * 8 + pair * 2 + c, 1), :]
                rows.append(jnp.broadcast_to(row >> 7, (8, 128)))
                hot = jnp.broadcast_to(row & 127, (128, 128)) == lanes
                hots.append(jnp.where(hot, 1.0, 0.0).astype(jnp.bfloat16))
            hot = jnp.concatenate(hots, axis=1)
            hot = jnp.concatenate([hot, hot, hot], axis=0)
            got = jnp.dot(tparts[...], hot, preferred_element_type=jnp.float32)
            for c in range(2):
                acc = got[0:8, c * 128 : (c + 1) * 128]
                for h in range(1, blocks):
                    piece = got[h * 8 : h * 8 + 8, c * 128 : (c + 1) * 128]
                    acc = jnp.where(rows[c] == h, piece, acc)
                start = pl.multiple_of((t * 8 + pair * 2 + c) * 8, 8)
                nodal[pl.ds(start, 8), :] = acc
        return carry

    lax.fori_loop(0, 8, step, 0)


def point_stage(coef, jac, weights, nodal, living, lame, shear, visc, grads, pushed, wsg, wpush, wleft, res):
    res[...] = jnp.zeros_like(res)

    def step(q, carry):
        base = q * 9
        w = jnp.where(living, weights[pl.ds(q, 8, stride=8), :], 0.0)
        jac_rows = [[jac[pl.ds(base + 3 * k + l, 8, stride=72), :] for l in range(3)] for k in range(3)]
        scaled = {}
        for k in range(3):
            for sm in range(2):
                for sn in range(2):
                    factor = coef[q * 12 + k * 4 + sm * 2 + sn]
                    scaled[k, sm, sn] = [jac_rows[k][l] * factor for l in range(3)]
        g = []
        for a in range(8):
            rows = []
            for l in range(3):
                total = None
                for k in range(3):
                    m, n = OTHERS[k]
                    term = scaled[k, (SIGNS[a][m] + 1) // 2, (SIGNS[a][n] + 1) // 2][l]
                    if total is None:
                        total = term if SIGNS[a][k] > 0 else -term
                    else:
                        total = total + term if SIGNS[a][k] > 0 else total - term
                rows.append(total)
            g.append(rows)
        for a in range(8):
            for l in range(3):
                grads[pl.ds(pl.multiple_of((q * 24 + a * 3 + l) * 8, 8), 8), :] = g[a][l]

        def gradient(first):
            rows = [[None] * 3 for _ in range(3)]
            for i in range(3):
                for a in range(8):
                    u = nodal[pl.ds(a * 8 + first + i, 8, stride=64), :]
                    for l in range(3):
                        term = u * g[a][l]
                        rows[i][l] = term if a == 0 else rows[i][l] + term
                rows[i][i] = rows[i][i] + 1.0
            return rows

        def right(f):
            return [f[0][l] * f[0][m] + f[1][l] * f[1][m] + f[2][l] * f[2][m] for l, m in SYM]

        old = right(gradient(3))
        f = gradient(0)
        new = right(f)
        strain = [0.5 * (new[s] - (1.0 if l == m else 0.0)) for s, (l, m) in enumerate(SYM)]
        change = [0.5 * (new[s] - old[s]) for s in range(6)]
        trace = lame * (strain[0] + strain[3] + strain[5])
        mu2, visc2 = 2.0 * shear, 2.0 * visc
        stress = []
        for s, (l, m) in enumerate(SYM):
            value = mu2 * strain[s] + visc2 * change[s]
            stress.append(w * (value + trace if l == m else value))
        modulus = w * (shear + visc)
        for s, (i, j) in enumerate(SYM):
            left = f[i][0] * f[j][0] + f[i][1] * f[j][1] + f[i][2] * f[j][2]
            wleft[pl.ds(pl.multiple_of((q * 6 + s) * 8, 8), 8), :] = modulus * left
        for a in range(8):
            sg = [
                stress[sym(l, 0)] * g[a][0] + stress[sym(l, 1)] * g[a][1] + stress[sym(l, 2)] * g[a][2]
                for l in range(3)
            ]
            for i in range(3):
                start = pl.multiple_of((q * 24 + a * 3 + i) * 8, 8)
                value = f[i][0] * g[a][0] + f[i][1] * g[a][1] + f[i][2] * g[a][2]
                pushed[pl.ds(start, 8), :] = value
                wpush[pl.ds(start, 8), :] = w * value
                wsg[pl.ds(start, 8), :] = sg[i]
                term = f[i][0] * sg[0] + f[i][1] * sg[1] + f[i][2] * sg[2]
                res[pl.ds((a * 3 + i) * 8, 8), :] += term
        return carry

    lax.fori_loop(0, 8, step, 0)


def pair_stage(lame, modulus, grads, pushed, wsg, wpush, wleft, blocks, vbase):
    def rows_of(ref, q, corner, width=24):
        return [
            ref[pl.ds(pl.multiple_of((q * width + corner * 3 + l) * 8, 8), 8), :] for l in range(3)
        ]

    def outer(a, carry):
        def inner(b, carry):
            prod = [None] * 9
            stretch = [None] * 6
            geo = None
            for q in range(8):
                ga = rows_of(grads, q, a)
                gb = rows_of(grads, q, b)
                sb = rows_of(wsg, q, b)
                pa = rows_of(wpush, q, a)
                pb = rows_of(pushed, q, b)
                metric = ga[0] * gb[0] + ga[1] * gb[1] + ga[2] * gb[2]
                bend = ga[0] * sb[0] + ga[1] * sb[1] + ga[2] * sb[2]
                geo = bend if q == 0 else geo + bend
                for i in range(3):
                    for j in range(3):
                        term = pa[i] * pb[j]
                        prod[3 * i + j] = term if q == 0 else prod[3 * i + j] + term
                for s in range(6):
                    term = metric * wleft[pl.ds((q * 6 + s) * 8, 8), :]
                    stretch[s] = term if q == 0 else stretch[s] + term
            for i in range(3):
                for j in range(3):
                    value = lame * prod[3 * i + j] + modulus * prod[3 * j + i] + stretch[sym(i, j)]
                    if i == j:
                        value = value + geo
                    first = pl.multiple_of(vbase + (a * 9 + 3 * i + j) * 64 + b * 8, 8)
                    blocks[pl.ds(first, 8), :] = value
                    second = pl.multiple_of(vbase + (b * 9 + 3 * j + i) * 64 + a * 8, 8)
                    blocks[pl.ds(second, 8), :] = value
            return carry

        return lax.fori_loop(a, 8, inner, carry)

    lax.fori_loop(0, 8, outer, 0)


def merge_stage(slots, sbase, blocks, vbase):
    def step(a, carry):
        rows = [slots[pl.ds(sbase + a * 8 + b, 8, stride=64), :] for b in range(8)]

        def at(ij, b):
            return pl.ds(pl.multiple_of(vbase + (a * 9 + ij) * 64 + b * 8, 8), 8)

        for early in range(7):
            sums = [blocks[at(ij, early), :] for ij in range(9)]
            for late in range(early + 1, 8):
                same = rows[early] == rows[late]
                for ij in range(9):
                    sums[ij] = sums[ij] + jnp.where(same, blocks[at(ij, late), :], 0.0)
            for ij in range(9):
                blocks[at(ij, early), :] = sums[ij]
        return carry

    lax.fori_loop(0, 8, step, 0)


def expand(code, slots, blocks, res, spread, turned, group_of):
    tile, corner = code >> 3, code & 7
    group, t = group_of(tile)
    sbase = pl.multiple_of((group * 8 + t) * 64 + corner * 8, 8)
    vbase = group * VROWS + corner * 576 + t
    lines = lax.broadcasted_iota(jnp.int32, (8, 128), 0)
    none = jnp.full((8, 128), 8, jnp.int32)
    found = [none] * 4
    for b in range(7, -1, -1):
        away = jnp.broadcast_to(slots[pl.ds(sbase + b, 1), :], (8, 128)) - lines
        found = [jnp.where(away == 8 * k, b, found[k]) for k in range(4)]
    valid = [f < 8 for f in found]
    found = [f & 7 for f in found]
    for ij in range(9):
        value = blocks[pl.ds(vbase + ij * 64, 8, stride=8), :]
        for k in range(4):
            picked = jnp.take_along_axis(value, found[k], axis=0, mode="promise_in_bounds")
            spread[27 * ij + 8 * k : 27 * ij + 8 * k + 8, :] = jnp.where(valid[k], picked, 0.0)
    spread[243:246, :] = res[pl.ds(group * 192 + corner * 24 + t, 3, stride=8), :]
    for half in range(2):
        turned[pl.ds(half, 128, stride=2), :] = spread[half * 128 : half * 128 + 128, :].T


def scatter(code, index, turned, accs):
    base = (code & 7) * ELEMS + (code >> 3) * 128
    for first in range(0, 128, WAYS):
        places = [pl.ds(index[base + first + v], 2) for v in range(WAYS)]
        sums = [
            accs[v][places[v], :] + turned[2 * (first + v) : 2 * (first + v) + 2, :] for v in range(WAYS)
        ]
        for v in range(WAYS):
            accs[v][places[v], :] = sums[v]


def run_units(units, count, spread, turned, accs, index, slots, blocks, res, group_of):
    for ref in spread:
        ref[240:, :] = jnp.zeros_like(ref[240:, :])
    turned[1][...] = jnp.zeros_like(turned[1])

    def step(turn, before):
        one = units[2 * turn]
        two = units[2 * turn + 1]
        expand(one, slots, blocks, res, spread[0], turned[0], group_of)
        scatter(before, index, turned[1], accs)
        expand(two, slots, blocks, res, spread[1], turned[1], group_of)
        scatter(one, index, turned[0], accs)
        return two

    last = lax.fori_loop(0, count // 2, step, units[0])
    scatter(last, index, turned[1], accs)


def materials_of(ids, materials):
    params = []
    for row in range(3):
        value = jnp.zeros((8, 128), jnp.float32)
        for m in range(8):
            value = jnp.where(ids == m, materials[row, m], value)
        params.append(value)
    return params


def zero(refs):
    for ref in refs:
        rows = ref.shape[0]

        def step(i, carry, ref=ref):
            ref[pl.ds(pl.multiple_of(i * 256, 256), 256), :] = jnp.zeros((256, 128), jnp.float32)
            return carry

        lax.fori_loop(0, rows // 256, step, 0)


def face_kernel(
    counts, flags, coef, materials, index, ids, disp, prev, ghost_blk, ghost_mer, ghost_ply,
    conn_hbm, slot_hbm, jac_hbm, weight_hbm,
    blocks, res, out_blk, out_mer, out_ply,
    conn, slots, jac, weights, nodal, table, tparts, grads, pushed, wsg, wpush, wleft,
    spread0, spread1, turned0, turned1, units, sems, *accs,
):
    copies = []
    for n, (src, dst, rows) in enumerate(
        [(conn_hbm, conn, 8), (slot_hbm, slots, 64), (jac_hbm, jac, 72), (weight_hbm, weights, 8)]
    ):
        copies += tile_copies(src, dst, rows, 8, 8, sems.at[n])
    for copy in copies:
        copy.start()
    table[...] = jnp.zeros_like(table)
    for h in range(16):
        table[h * 8 : h * 8 + 3, :] = disp[:, h * 128 : h * 128 + 128]
        table[h * 8 + 3 : h * 8 + 6, :] = prev[:, h * 128 : h * 128 + 128]
    h = 16
    for ghost, count in ((ghost_blk, 4), (ghost_mer, 2), (ghost_ply, 1)):
        for n in range(count):
            table[h * 8 : h * 8 + 6, :] = ghost[:, n * 128 : n * 128 + 128]
            h += 1
    split_table(table, tparts)
    zero(accs)
    for copy in copies:
        copy.wait()
    gather_nodal(conn, tparts, nodal, 23)
    lame, shear, visc = materials_of(ids[...], materials)
    tile = lax.broadcasted_iota(jnp.int32, (8, 128), 0)
    lane = lax.broadcasted_iota(jnp.int32, (8, 128), 1)
    living = (tile > 0) | (lane + 1024 < counts[0])
    point_stage(coef, jac, weights, nodal, living, lame, shear, visc, grads, pushed, wsg, wpush, wleft, res)
    pair_stage(lame, shear + visc, grads, pushed, wsg, wpush, wleft, blocks, 0)
    merge_stage(slots, 0, blocks, 0)
    for n in range(16):
        units[n] = (12 + n // 4) * 8 + 4 + n % 4
    count = 16 + 0 * flags[0]

    @pl.when(flags[0] > 0)
    def _():
        for n in range(8):
            units[16 + n] = (10 + n // 4) * 8 + 4 + n % 4

    count = count + 8 * flags[0]

    @pl.when(flags[1] > 0)
    def _():
        for n in range(4):
            units[count + n] = 9 * 8 + 4 + n % 4

    count = count + 4 * flags[1]
    run_units(
        units, count, (spread0, spread1), (turned0, turned1), accs, index, slots, blocks, res,
        lambda tile: (0, tile - 8),
    )
    first = 0
    for out in (out_blk, out_mer, out_ply):
        rows = out.shape[0]
        total = accs[0][first : first + rows, :]
        for acc in accs[1:]:
            total = total + acc[first : first + rows, :]
        out[...] = total
        first += rows


def own_kernel(
    counts, flags, coef, materials, index, ids, disp, prev, load,
    conn_hbm, slot_hbm, jac_hbm, weight_hbm, blocks_hbm, res_hbm,
    residual, tangent,
    conn, slots, jac, weights, nodal, table, tparts, grads, pushed, wsg, wpush, wleft,
    spread0, spread1, turned0, turned1, blocks, res, units, sems, *accs,
):
    copies = []
    for n, (src, dst, rows, count) in enumerate(
        [(conn_hbm, conn, 8, 8), (jac_hbm, jac, 72, 8), (weight_hbm, weights, 8, 8), (slot_hbm, slots, 64, 16)]
    ):
        copies += tile_copies(src, dst, rows, 0, count, sems.at[n])
    copies.append(pltpu.make_async_copy(blocks_hbm, blocks.at[pl.ds(VROWS, VROWS), :], sems.at[4, 0]))
    copies.append(pltpu.make_async_copy(res_hbm, res.at[pl.ds(192, 192), :], sems.at[4, 1]))
    for copy in copies:
        copy.start()
    table[...] = jnp.zeros_like(table)
    for h in range(16):
        table[h * 8 : h * 8 + 3, :] = disp[:, h * 128 : h * 128 + 128]
        table[h * 8 + 3 : h * 8 + 6, :] = prev[:, h * 128 : h * 128 + 128]
    split_table(table, tparts)
    zero(accs)
    for copy in copies:
        copy.wait()
    gather_nodal(conn, tparts, nodal, 16)
    lame, shear, visc = materials_of(ids[...], materials)
    tile = lax.broadcasted_iota(jnp.int32, (8, 128), 0)
    lane = lax.broadcasted_iota(jnp.int32, (8, 128), 1)
    living = tile * 128 + lane < counts[0]
    point_stage(
        coef, jac, weights, nodal, living, lame, shear, visc, grads, pushed, wsg, wpush, wleft,
        res.at[pl.ds(0, 192), :],
    )
    pair_stage(lame, shear + visc, grads, pushed, wsg, wpush, wleft, blocks, 0)
    merge_stage(slots, 0, blocks, 0)
    inner = (counts[0] + 127) // 128

    def put(tile, first, last, count):
        for corner in range(first, last):
            units[count + corner - first] = tile * 8 + corner
        return count + last - first

    count = lax.fori_loop(0, inner, lambda tile, n: put(tile, 0, 8, n), 0)
    count = lax.fori_loop(9, 16, lambda tile, n: put(tile, 0, 4, n), count)
    count = lax.fori_loop(9, jnp.where(flags[1] > 0, 9, 10), lambda tile, n: put(tile, 4, 8, n), count)
    count = lax.fori_loop(10, jnp.where(flags[0] > 0, 10, 12), lambda tile, n: put(tile, 4, 8, n), count)
    run_units(
        units, count, (spread0, spread1), (turned0, turned1), accs, index, slots, blocks, res,
        lambda tile: (tile >> 3, tile & 7),
    )

    def finish(n, carry):
        columns = pl.ds(pl.multiple_of(n * 128, 128), 128)
        for half in range(2):
            total = accs[0][pl.ds(n * 256 + half, 128, stride=2), :]
            for acc in accs[1:]:
                total = total + acc[pl.ds(n * 256 + half, 128, stride=2), :]
            total = total.T
            if half == 0:
                tangent[0:128, columns] = total
            else:
                tangent[128:243, columns] = total[0:115]
                residual[:, columns] = total[115:118] - load[:, columns]
        return carry

    lax.fori_loop(0, 16, finish, 0)


def back_kernel(residual, tangent, back_blk, back_mer, back_ply, residual_out, tangent_out):
    tile = pl.program_id(0)
    for half in range(2):
        rows = pl.ds(half, 128, stride=2)
        total = back_blk[rows, :]
        total = total + jnp.where(tile < 2, back_mer[rows, :], 0.0)
        total = total + jnp.where(tile < 1, back_ply[rows, :], 0.0)
        total = total.T
        if half == 0:
            tangent_out[0:128, :] = tangent[0:128, :] + total
        else:
            tangent_out[128:243, :] = tangent[128:243, :] + total[0:115]
            residual_out[...] = residual[...] + total[115:118]


def scratch_of(table_rows, slot_tiles):
    f32, i32 = jnp.float32, jnp.int32
    return [
        pltpu.VMEM((64, 128), i32),
        pltpu.VMEM((slot_tiles * 64, 128), i32),
        pltpu.VMEM((8 * 72, 128), f32),
        pltpu.VMEM((64, 128), f32),
        pltpu.VMEM((512, 128), f32),
        pltpu.VMEM((table_rows, 128), f32),
        pltpu.VMEM((table_rows, 384), jnp.bfloat16),
        pltpu.VMEM((8 * 24 * 8, 128), f32),
        pltpu.VMEM((8 * 24 * 8, 128), f32),
        pltpu.VMEM((8 * 24 * 8, 128), f32),
        pltpu.VMEM((8 * 24 * 8, 128), f32),
        pltpu.VMEM((8 * 6 * 8, 128), f32),
        pltpu.VMEM((256, 128), f32),
        pltpu.VMEM((256, 128), f32),
        pltpu.VMEM((256, 128), f32),
        pltpu.VMEM((256, 128), f32),
    ]


def body(
    connectivity,
    slot_map,
    material_ids,
    element_counts,
    inverse_jacobians,
    quadrature_weights,
    materials,
    displacement,
    previous,
    load,
):
    f32 = jnp.float32
    state = jnp.concatenate([displacement[:, :512], previous[:, :512]], axis=0)
    size = lax.axis_size("blk")
    ghost_blk = lax.ppermute(state, "blk", [((i + 1) % size, i) for i in range(size)])
    ghost_mer = lax.ppermute(state, "mer", [(i + 1, i) for i in range(lax.axis_size("mer") - 1)])
    ghost_ply = lax.ppermute(state, "ply", [(i + 1, i) for i in range(lax.axis_size("ply") - 1)])
    index = (jnp.where(connectivity >= NODES, connectivity - NODES, connectivity) * 2).reshape(-1)
    flags = jnp.stack(
        [
            (lax.axis_index("mer") < lax.axis_size("mer") - 1).astype(jnp.int32),
            (lax.axis_index("ply") < lax.axis_size("ply") - 1).astype(jnp.int32),
        ]
    )
    coef = jnp.asarray(shape_factors(), f32)
    ids = material_ids.reshape(TILES, 128)
    smem = pl.BlockSpec(memory_space=pltpu.SMEM)
    vmem = pl.BlockSpec(memory_space=pltpu.VMEM)
    hbm = pl.BlockSpec(memory_space=pl.ANY)
    half = lambda n: pl.BlockSpec((8, 128), lambda i: (n, 0))
    params = pltpu.CompilerParams(vmem_limit_bytes=VMEM)
    blocks, res, face_blk, face_mer, face_ply = pl.pallas_call(
        face_kernel,
        grid=(1,),
        out_shape=[
            jax.ShapeDtypeStruct((VROWS, 128), f32),
            jax.ShapeDtypeStruct((192, 128), f32),
            jax.ShapeDtypeStruct((1024, 128), f32),
            jax.ShapeDtypeStruct((512, 128), f32),
            jax.ShapeDtypeStruct((256, 128), f32),
        ],
        in_specs=[smem] * 5 + [half(1)] + [vmem] * 5 + [hbm] * 4,
        out_specs=[vmem] * 5,
        scratch_shapes=scratch_of(184, 8)
        + [pltpu.SMEM((128,), jnp.int32), pltpu.SemaphoreType.DMA((4, 8))]
        + [pltpu.VMEM((1792, 128), f32)] * WAYS,
        compiler_params=params,
        name="faces",
    )(
        element_counts, flags, coef, materials, index, ids, displacement, previous,
        ghost_blk, ghost_mer, ghost_ply, connectivity, slot_map, inverse_jacobians, quadrature_weights,
    )
    back_blk = lax.ppermute(face_blk, "blk", [(i, (i + 1) % size) for i in range(size)])
    back_mer = lax.ppermute(face_mer, "mer", [(i, i + 1) for i in range(lax.axis_size("mer") - 1)])
    back_ply = lax.ppermute(face_ply, "ply", [(i, i + 1) for i in range(lax.axis_size("ply") - 1)])
    residual, tangent = pl.pallas_call(
        own_kernel,
        grid=(1,),
        out_shape=[
            jax.ShapeDtypeStruct((3, NODES), f32),
            jax.ShapeDtypeStruct((9 * SLOTS, NODES), f32),
        ],
        in_specs=[smem] * 5 + [half(0)] + [vmem] * 3 + [hbm] * 6,
        out_specs=[vmem] * 2,
        scratch_shapes=scratch_of(128, 16)
        + [
            pltpu.VMEM((2 * VROWS, 128), f32),
            pltpu.VMEM((384, 128), f32),
            pltpu.SMEM((160,), jnp.int32),
            pltpu.SemaphoreType.DMA((5, 16)),
        ]
        + [pltpu.VMEM((2 * NODES, 128), f32)] * WAYS,
        compiler_params=params,
        cost_estimate=pl.CostEstimate(flops=10**8, bytes_accessed=10**8, transcendentals=0),
        name="own",
    )(
        element_counts, flags, coef, materials, index, ids, displacement, previous, load,
        connectivity, slot_map, inverse_jacobians, quadrature_weights, blocks, res,
    )
    column = lambda rows: pl.BlockSpec((rows, 128), lambda i: (0, i))
    residual, tangent = pl.pallas_call(
        back_kernel,
        grid=(4,),
        out_shape=[
            jax.ShapeDtypeStruct((3, NODES), f32),
            jax.ShapeDtypeStruct((9 * SLOTS, NODES), f32),
        ],
        in_specs=[
            column(3),
            column(243),
            pl.BlockSpec((256, 128), lambda i: (i, 0)),
            pl.BlockSpec((256, 128), lambda i: (jnp.minimum(i, 1), 0)),
            pl.BlockSpec((256, 128), lambda i: (0, 0)),
        ],
        out_specs=[column(3), column(243)],
        input_output_aliases={0: 0, 1: 1},
        compiler_params=params,
        name="back",
    )(residual, tangent, back_blk, back_mer, back_ply)
    return residual, tangent


def solution(mesh):
    return jax.shard_map(
        body,
        mesh=mesh,
        in_specs=(
            P(None, ("blk", "mer", "ply")),
            P(None, ("blk", "mer", "ply")),
            P(("blk", "mer", "ply")),
            P(("blk", "mer", "ply")),
            P(None, ("blk", "mer", "ply")),
            P(None, ("blk", "mer", "ply")),
            P(),
            P(None, ("blk", "mer", "ply")),
            P(None, ("blk", "mer", "ply")),
            P(None, ("blk", "mer", "ply")),
        ),
        out_specs=(P(None, ("blk", "mer", "ply")), P(None, ("blk", "mer", "ply"))),
        check_vma=False,
    )
```

```python
import math

import jax
import jax.numpy as jnp
from jax import lax
from jax.experimental import pallas as pl
from jax.experimental.pallas import tpu as pltpu
from jax.sharding import PartitionSpec as P

SLOTS = 27
NODES = 2048
ELEMS = 2048
TILES = 16
WAYS = 8
VROWS = 8 * 9 * 64
VMEM = 60 * 1024 * 1024
AHEAD = 3

SIGNS = [
    [-1, -1, -1],
    [1, -1, -1],
    [1, 1, -1],
    [-1, 1, -1],
    [-1, -1, 1],
    [1, -1, 1],
    [1, 1, 1],
    [-1, 1, 1],
]
OTHERS = [(1, 2), (0, 2), (0, 1)]
SYM = [(0, 0), (0, 1), (0, 2), (1, 1), (1, 2), (2, 2)]


def shifted(value, axis, steps):
    count = lax.axis_size(axis)
    pairs = [(source, (source + steps) % count) for source in range(count)]
    return lax.ppermute(value, axis, pairs)


def sym(i, j):
    return SYM.index((min(i, j), max(i, j)))


def shape_factors(q):
    bits = [(q ^ (q >> 1)) & 1, (q >> 1) & 1, q >> 2]
    plus, minus = 1.0 + 1.0 / math.sqrt(3.0), 1.0 - 1.0 / math.sqrt(3.0)
    table = {}
    for k in range(3):
        m, n = OTHERS[k]
        for sm in range(2):
            for sn in range(2):
                like = (bits[m] == sm).astype(jnp.int32) + (bits[n] == sn).astype(jnp.int32)
                table[k, sm, sn] = jnp.where(
                    like == 2, plus * plus / 8.0, jnp.where(like == 1, plus * minus / 8.0, minus * minus / 8.0)
                )
    return table


def tiles_first(x):
    rows, columns = x.shape
    x = x.reshape(rows // 8, 8, columns // 128, 128).transpose(0, 2, 1, 3)
    return x.reshape(rows * columns // 128, 128)


def half_copies(src, dst, group, count, sem):
    return [
        pltpu.make_async_copy(
            src.at[pl.ds(n * 128 + group * 64, 64), :], dst.at[pl.ds(n * 64, 64), :], sem.at[n]
        )
        for n in range(count)
    ]


def split_table(table, tparts):
    value = table[...]
    high = value.astype(jnp.bfloat16)
    rest = value - high.astype(jnp.float32)
    mid = rest.astype(jnp.bfloat16)
    low = (rest - mid.astype(jnp.float32)).astype(jnp.bfloat16)
    tparts[:, 0:128] = high
    tparts[:, 128:256] = mid
    tparts[:, 256:384] = low


def gather_nodal(conn, tparts, nodal, blocks):
    lanes = lax.broadcasted_iota(jnp.int32, (128, 128), 0)

    def step(t, carry):
        for pair in range(4):
            rows = []
            hots = []
            for c in range(2):
                row = conn[pl.ds(t * 8 + pair * 2 + c, 1), :]
                rows.append(jnp.broadcast_to(row >> 7, (8, 128)))
                hot = jnp.broadcast_to(row & 127, (128, 128)) == lanes
                hots.append(jnp.where(hot, 1.0, 0.0).astype(jnp.bfloat16))
            hot = jnp.concatenate(hots, axis=1)
            hot = jnp.concatenate([hot, hot, hot], axis=0)
            got = jnp.dot(tparts[...], hot, preferred_element_type=jnp.float32)
            for c in range(2):
                acc = got[0:8, c * 128 : (c + 1) * 128]
                for h in range(1, blocks):
                    piece = got[h * 8 : h * 8 + 8, c * 128 : (c + 1) * 128]
                    acc = jnp.where(rows[c] == h, piece, acc)
                start = pl.multiple_of((t * 8 + pair * 2 + c) * 8, 8)
                nodal[pl.ds(start, 8), :] = acc
        return carry

    lax.fori_loop(0, 8, step, 0)


def point_stage(jac, weights, nodal, living, lame, shear, visc, grads, pushed, wsg, wpush, wleft, res):
    res[...] = jnp.zeros_like(res)

    def step(q, carry):
        base = q * 9
        w = jnp.where(living, weights[pl.ds(q, 8, stride=8), :], 0.0)
        jac_rows = []
        for k in range(3):
            rows = [base + 3 * k + l for l in range(3)]
            jac_rows.append([jac[pl.ds((row >> 3) * 64 + (row & 7), 8, stride=8), :] for row in rows])
        scaled = {
            (k, sm, sn): [jac_rows[k][l] * factor for l in range(3)]
            for (k, sm, sn), factor in shape_factors(q).items()
        }
        g = []
        for a in range(8):
            rows = []
            for l in range(3):
                total = None
                for k in range(3):
                    m, n = OTHERS[k]
                    term = scaled[k, (SIGNS[a][m] + 1) // 2, (SIGNS[a][n] + 1) // 2][l]
                    if total is None:
                        total = term if SIGNS[a][k] > 0 else -term
                    else:
                        total = total + term if SIGNS[a][k] > 0 else total - term
                rows.append(total)
            g.append(rows)
        for a in range(8):
            for l in range(3):
                grads[pl.ds(pl.multiple_of((q * 24 + a * 3 + l) * 8, 8), 8), :] = g[a][l]

        def gradient(first):
            rows = [[None] * 3 for _ in range(3)]
            for i in range(3):
                for a in range(8):
                    u = nodal[pl.ds(a * 8 + first + i, 8, stride=64), :]
                    for l in range(3):
                        term = u * g[a][l]
                        rows[i][l] = term if a == 0 else rows[i][l] + term
                rows[i][i] = rows[i][i] + 1.0
            return rows

        def right(f):
            return [f[0][l] * f[0][m] + f[1][l] * f[1][m] + f[2][l] * f[2][m] for l, m in SYM]

        old = right(gradient(3))
        f = gradient(0)
        new = right(f)
        strain = [0.5 * (new[s] - (1.0 if l == m else 0.0)) for s, (l, m) in enumerate(SYM)]
        change = [0.5 * (new[s] - old[s]) for s in range(6)]
        trace = lame * (strain[0] + strain[3] + strain[5])
        mu2, visc2 = 2.0 * shear, 2.0 * visc
        stress = []
        for s, (l, m) in enumerate(SYM):
            value = mu2 * strain[s] + visc2 * change[s]
            stress.append(w * (value + trace if l == m else value))
        modulus = w * (shear + visc)
        for s, (i, j) in enumerate(SYM):
            left = f[i][0] * f[j][0] + f[i][1] * f[j][1] + f[i][2] * f[j][2]
            wleft[pl.ds(pl.multiple_of((q * 6 + s) * 8, 8), 8), :] = modulus * left
        for a in range(8):
            sg = [
                stress[sym(l, 0)] * g[a][0] + stress[sym(l, 1)] * g[a][1] + stress[sym(l, 2)] * g[a][2]
                for l in range(3)
            ]
            for i in range(3):
                start = pl.multiple_of((q * 24 + a * 3 + i) * 8, 8)
                value = f[i][0] * g[a][0] + f[i][1] * g[a][1] + f[i][2] * g[a][2]
                pushed[pl.ds(start, 8), :] = value
                wpush[pl.ds(start, 8), :] = w * value
                wsg[pl.ds(start, 8), :] = sg[i]
                term = f[i][0] * sg[0] + f[i][1] * sg[1] + f[i][2] * sg[2]
                res[pl.ds((a * 3 + i) * 8, 8), :] += term
        return carry

    lax.fori_loop(0, 8, step, 0)


def pair_stage(lame, modulus, grads, pushed, wsg, wpush, wleft, blocks, vbase):
    def rows_of(ref, q, corner, width=24):
        return [
            ref[pl.ds(pl.multiple_of((q * width + corner * 3 + l) * 8, 8), 8), :] for l in range(3)
        ]

    def outer(a, carry):
        def inner(b, carry):
            prod = [None] * 9
            stretch = [None] * 6
            geo = None
            for q in range(8):
                ga = rows_of(grads, q, a)
                gb = rows_of(grads, q, b)
                sb = rows_of(wsg, q, b)
                pa = rows_of(wpush, q, a)
                pb = rows_of(pushed, q, b)
                metric = ga[0] * gb[0] + ga[1] * gb[1] + ga[2] * gb[2]
                bend = ga[0] * sb[0] + ga[1] * sb[1] + ga[2] * sb[2]
                geo = bend if q == 0 else geo + bend
                for i in range(3):
                    for j in range(3):
                        term = pa[i] * pb[j]
                        prod[3 * i + j] = term if q == 0 else prod[3 * i + j] + term
                for s in range(6):
                    term = metric * wleft[pl.ds((q * 6 + s) * 8, 8), :]
                    stretch[s] = term if q == 0 else stretch[s] + term
            for i in range(3):
                for j in range(3):
                    value = lame * prod[3 * i + j] + modulus * prod[3 * j + i] + stretch[sym(i, j)]
                    if i == j:
                        value = value + geo
                    first = pl.multiple_of(vbase + (a * 9 + 3 * i + j) * 64 + b * 8, 8)
                    blocks[pl.ds(first, 8), :] = value
                    second = pl.multiple_of(vbase + (b * 9 + 3 * j + i) * 64 + a * 8, 8)
                    blocks[pl.ds(second, 8), :] = value
            return carry

        return lax.fori_loop(a, 8, inner, carry)

    lax.fori_loop(0, 8, outer, 0)


def merge_stage(slots, tiles, blocks):
    def step(a, carry):
        rows = [slots[pl.ds(a * tiles * 8 + b, 8, stride=8), :] for b in range(8)]

        def at(ij, b):
            return pl.ds(pl.multiple_of((a * 9 + ij) * 64 + b * 8, 8), 8)

        for early in range(7):
            sums = [blocks[at(ij, early), :] for ij in range(9)]
            for late in range(early + 1, 8):
                same = rows[early] == rows[late]
                for ij in range(9):
                    sums[ij] = sums[ij] + jnp.where(same, blocks[at(ij, late), :], 0.0)
            for ij in range(9):
                blocks[at(ij, early), :] = sums[ij]
        return carry

    lax.fori_loop(0, 8, step, 0)


def expand(corner, group, t, slots, blocks, res, spread):
    sbase = pl.multiple_of((corner * (slots.shape[0] // 64) + group * 8 + t) * 8, 8)
    vbase = group * VROWS + corner * 576 + t
    lines = lax.broadcasted_iota(jnp.int32, (8, 128), 0)
    none = jnp.full((8, 128), 8, jnp.int32)
    found = [none] * 4
    for b in range(7, -1, -1):
        away = jnp.broadcast_to(slots[pl.ds(sbase + b, 1), :], (8, 128)) - lines
        found = [jnp.where(away == 8 * k, b, found[k]) for k in range(4)]
    valid = [f < 8 for f in found]
    found = [f & 7 for f in found]
    for ij in range(9):
        value = blocks[pl.ds(vbase + ij * 64, 8, stride=8), :]
        for k in range(4):
            picked = jnp.take_along_axis(value, found[k], axis=0, mode="promise_in_bounds")
            spread[27 * ij + 8 * k : 27 * ij + 8 * k + 8, :] = jnp.where(valid[k], picked, 0.0)
    spread[243:246, :] = res[pl.ds(group * 192 + corner * 24 + t, 3, stride=8), :]


def turn(spread, turned):
    for half in range(2):
        turned[pl.ds(half, 128, stride=2), :] = spread[half * 128 : half * 128 + 128, :].T


def scatter(index, unit, turned, accs):
    for first in range(0, 128, WAYS):
        places = [pl.ds(index[unit, first + v], 2) for v in range(WAYS)]
        sums = [
            accs[v][places[v], :] + turned[2 * (first + v) : 2 * (first + v) + 2, :] for v in range(WAYS)
        ]
        for v in range(WAYS):
            accs[v][places[v], :] = sums[v]


def run_quads(quads, count, spread, turned, accs, rows, index, sems, slots, blocks, res, first_tile):
    def fetch(quad, buffer):
        return pltpu.make_async_copy(rows.at[quads[quad]], index[buffer], sems.at[buffer])

    first = pltpu.make_async_copy(rows.at[quads[0]], index[AHEAD], sems.at[AHEAD])
    first.start()
    for n in range(AHEAD):
        fetch(n, n).start()
    for ref in spread:
        ref[...] = jnp.zeros_like(ref)
    turned[0][...] = jnp.zeros_like(turned[0])
    first.wait()

    def step(quad, carry):
        code = quads[quad]
        tile, corner = code >> 1, (code & 1) * 4
        group, t = (tile - first_tile) >> 3, tile & 7

        def work(now):
            before = (now - 1) % (AHEAD + 1)
            fetch(quad, now).wait()
            for n in range(4):
                expand(corner + n, group, t, slots, blocks, res, spread[n % 2])
                turn(spread[(n + 1) % 2], turned[(n + 1) % 2])
                if n < 2:
                    scatter(index[before], n + 2, turned[n % 2], accs)
                else:
                    scatter(index[now], n - 2, turned[n % 2], accs)

            @pl.when(quad + AHEAD < count)
            def _():
                fetch(quad + AHEAD, before).start()

        for now in range(AHEAD + 1):
            pl.when(lax.rem(quad, AHEAD + 1) == now)(lambda now=now: work(now))
        return carry

    lax.fori_loop(0, count, step, 0)
    turn(spread[1], turned[1])
    for now in range(AHEAD + 1):

        @pl.when(lax.rem(count - 1, AHEAD + 1) == now)
        def _(now=now):
            scatter(index[now], 2, turned[0], accs)
            scatter(index[now], 3, turned[1], accs)


def materials_of(ids, materials):
    params = []
    for row in range(3):
        value = jnp.zeros((8, 128), jnp.float32)
        for m in range(8):
            value = jnp.where(ids == m, materials[row, m], value)
        params.append(value)
    return params


def zero(refs):
    for ref in refs:
        rows = ref.shape[0]

        def step(i, carry, ref=ref):
            ref[pl.ds(pl.multiple_of(i * 256, 256), 256), :] = jnp.zeros((256, 128), jnp.float32)
            return carry

        lax.fori_loop(0, rows // 256, step, 0)


def table_rows(table, state, blocks, first):
    for h in range(blocks):
        start = (first + h) * 8
        table[start : start + 6, :] = state[:, h * 128 : h * 128 + 128]


def scatter_rows(conn, rows, tiles, first_tile):
    for tile in range(tiles):
        for half in range(2):
            node = conn[tile * 8 + half * 4 : tile * 8 + half * 4 + 4, :]
            node = jnp.where(node >= NODES, node - NODES, node)
            rows[(first_tile + tile) * 2 + half] = node * 2


def started(copies):
    for copy in copies:
        copy.start()
    return copies


def done(copies):
    for copy in copies:
        copy.wait()


def face_kernel(
    counts_hbm, materials_hbm, ids_hbm, state_hbm, blk_hbm, mer_hbm, ply_hbm,
    conn_hbm, slot_hbm, jac_hbm, weight_hbm,
    blocks_out, res_out, out_blk, out_mer, out_ply,
    counts, materials, ids, state, ghost_blk, ghost_mer, ghost_ply, sum_blk, sum_mer, sum_ply,
    conn, slots, jac, weights, nodal, table, tparts, grads, pushed, wsg, wpush, wleft,
    spread0, spread1, turned0, turned1, rows, blocks, res, quads, sems, index_sems, *more,
):
    index, accs = more[: AHEAD + 1], more[AHEAD + 1 :]
    nodes = started(
        [
            pltpu.make_async_copy(src, dst, sems.at[4, n])
            for n, (src, dst) in enumerate(
                [(state_hbm, state), (blk_hbm, ghost_blk), (mer_hbm, ghost_mer), (ply_hbm, ghost_ply)]
            )
        ]
        + half_copies(conn_hbm, conn, 1, 1, sems.at[0])
    )
    points = started(
        [
            pltpu.make_async_copy(ids_hbm.at[pl.ds(8, 8), :], ids, sems.at[4, 4]),
            pltpu.make_async_copy(counts_hbm, counts, sems.at[4, 7]),
            pltpu.make_async_copy(materials_hbm, materials, sems.at[4, 8]),
        ]
        + half_copies(weight_hbm, weights, 1, 1, sems.at[1])
        + half_copies(jac_hbm, jac, 1, 9, sems.at[2])
    )
    pairs = started(half_copies(slot_hbm, slots, 1, 8, sems.at[3]))
    table[...] = jnp.zeros_like(table)
    zero(accs)
    done(nodes)
    table_rows(table, state, 16, 0)
    table_rows(table, ghost_blk, 4, 16)
    table_rows(table, ghost_mer, 2, 20)
    table_rows(table, ghost_ply, 1, 22)
    split_table(table, tparts)
    scatter_rows(conn, rows, 8, 8)
    gather_nodal(conn, tparts, nodal, 23)
    done(points)
    lame, shear, visc = materials_of(ids[...], materials)
    tile = lax.broadcasted_iota(jnp.int32, (8, 128), 0)
    lane = lax.broadcasted_iota(jnp.int32, (8, 128), 1)
    living = (tile > 0) | (lane + 1024 < counts[0])
    point_stage(jac, weights, nodal, living, lame, shear, visc, grads, pushed, wsg, wpush, wleft, res)
    pair_stage(lame, shear + visc, grads, pushed, wsg, wpush, wleft, blocks, 0)
    done(pairs)
    merge_stage(slots, 8, blocks)
    results = started(
        [
            pltpu.make_async_copy(blocks, blocks_out, sems.at[4, 5]),
            pltpu.make_async_copy(res, res_out, sems.at[4, 6]),
        ]
    )
    mer = (lax.axis_index("mer") < lax.axis_size("mer") - 1).astype(jnp.int32)
    ply = (lax.axis_index("ply") < lax.axis_size("ply") - 1).astype(jnp.int32)
    for n in range(4):
        quads[n] = (12 + n) * 2 + 1
    for n in range(2):
        quads[4 + n] = (10 + n) * 2 + 1
    quads[4 + 2 * mer] = 9 * 2 + 1
    count = 4 + 2 * mer + ply
    run_quads(
        quads, count, (spread0, spread1), (turned0, turned1), accs, rows, index, index_sems,
        slots, blocks, res, 8,
    )
    first = 0
    for n, (part, out) in enumerate([(sum_blk, out_blk), (sum_mer, out_mer), (sum_ply, out_ply)]):
        size = part.shape[0]
        total = accs[0][first : first + size, :]
        for acc in accs[1:]:
            total = total + acc[first : first + size, :]
        part[...] = total
        results += started([pltpu.make_async_copy(part, out, sems.at[4, 9 + n])])
        first += size
    done(results)


def own_kernel(
    counts_hbm, materials_hbm, ids_hbm, state_hbm, load_hbm,
    conn_hbm, slot_hbm, jac_hbm, weight_hbm, blocks_hbm, res_hbm,
    residual_out, tangent_out, raw_out,
    counts, materials, ids, state, load, residual, tangent, raw,
    conn, slots, jac, weights, nodal, table, tparts, grads, pushed, wsg, wpush, wleft,
    spread0, spread1, turned0, turned1, rows, blocks, res, quads, sems, index_sems, *more,
):
    index, accs = more[: AHEAD + 1], more[AHEAD + 1 :]
    nodes = started(
        [pltpu.make_async_copy(state_hbm, state, sems.at[4, 0])]
        + [pltpu.make_async_copy(conn_hbm, conn, sems.at[0, 0])]
    )
    points = started(
        [
            pltpu.make_async_copy(ids_hbm.at[pl.ds(0, 8), :], ids, sems.at[4, 1]),
            pltpu.make_async_copy(counts_hbm, counts, sems.at[4, 12]),
            pltpu.make_async_copy(materials_hbm, materials, sems.at[4, 13]),
        ]
        + half_copies(weight_hbm, weights, 0, 1, sems.at[1])
        + half_copies(jac_hbm, jac, 0, 9, sems.at[2])
    )
    pairs = started([pltpu.make_async_copy(slot_hbm, slots, sems.at[3, 0])])
    units = started(
        [
            pltpu.make_async_copy(blocks_hbm, blocks.at[pl.ds(VROWS, VROWS), :], sems.at[4, 2]),
            pltpu.make_async_copy(res_hbm, res.at[pl.ds(192, 192), :], sems.at[4, 3]),
            pltpu.make_async_copy(load_hbm, load, sems.at[4, 4]),
        ]
    )
    table[...] = jnp.zeros_like(table)
    zero(accs)
    done(nodes)
    table_rows(table, state, 16, 0)
    split_table(table, tparts)
    scatter_rows(conn, rows, 16, 0)
    gather_nodal(conn, tparts, nodal, 16)
    done(points)
    lame, shear, visc = materials_of(ids[...], materials)
    tile = lax.broadcasted_iota(jnp.int32, (8, 128), 0)
    lane = lax.broadcasted_iota(jnp.int32, (8, 128), 1)
    living = tile * 128 + lane < counts[0]
    point_stage(
        jac, weights, nodal, living, lame, shear, visc, grads, pushed, wsg, wpush, wleft,
        res.at[pl.ds(0, 192), :],
    )
    pair_stage(lame, shear + visc, grads, pushed, wsg, wpush, wleft, blocks, 0)
    done(pairs)
    merge_stage(slots, 16, blocks)
    done(units)

    def put(tile, halves, count):
        for n, half in enumerate(halves):
            quads[count + n] = tile * 2 + half
        return count + len(halves)

    has_mer = lax.axis_index("mer") < lax.axis_size("mer") - 1
    has_ply = lax.axis_index("ply") < lax.axis_size("ply") - 1
    count = 0
    for tile in range(9, 16):
        count = put(tile, (0,), count)
    count = lax.fori_loop(0, (counts[0] + 127) // 128, lambda tile, n: put(tile, (0, 1), n), count)
    count = lax.fori_loop(9, jnp.where(has_ply, 9, 10), lambda tile, n: put(tile, (1,), n), count)
    count = lax.fori_loop(10, jnp.where(has_mer, 10, 12), lambda tile, n: put(tile, (1,), n), count)
    run_quads(
        quads, count, (spread0, spread1), (turned0, turned1), accs, rows, index, index_sems,
        slots, blocks, res, 0,
    )

    def add_up(part):
        total = accs[0][part, :]
        for acc in accs[1:]:
            total = total + acc[part, :]
        return total

    for n in range(4):
        raw[n * 256 : n * 256 + 256, :] = add_up(pl.ds(n * 256, 256))
    results = started([pltpu.make_async_copy(raw, raw_out, sems.at[4, 5])])

    def finish(step, carry):
        for k in range(2):
            n = 4 + step * 2 + k
            columns = pl.ds(pl.multiple_of(n * 128, 128), 128)
            tangent[0:128, columns] = add_up(pl.ds(n * 256, 128, stride=2)).T
            total = add_up(pl.ds(n * 256 + 1, 128, stride=2)).T
            tangent[128:243, columns] = total[0:115]
            residual[:, columns] = total[115:118] - load[:, columns]
        return carry

    for part in range(3):
        lax.fori_loop(part * 2, part * 2 + 2, finish, 0)
        columns = pl.ds(512 + part * 512, 512)
        results += started(
            [
                pltpu.make_async_copy(tangent.at[:, columns], tangent_out.at[:, columns], sems.at[4, 6 + part]),
                pltpu.make_async_copy(residual.at[:, columns], residual_out.at[:, columns], sems.at[4, 9 + part]),
            ]
        )
    done(results)


def back_kernel(
    residual_in, tangent_in, raw_hbm, blk_hbm, mer_hbm, ply_hbm, load_hbm, residual_out, tangent_out,
    raw, blk, mer, ply, load, residual, tangent, sems,
):
    del residual_in, tangent_in
    columns = pl.ds(0, 512)
    done(
        started(
            [
                pltpu.make_async_copy(src, dst, sems.at[n])
                for n, (src, dst) in enumerate(
                    [(raw_hbm, raw), (blk_hbm, blk), (mer_hbm, mer), (ply_hbm, ply), (load_hbm.at[:, columns], load)]
                )
            ]
        )
    )
    results = []
    for n in range(4):
        place = pl.ds(n * 128, 128)
        for half in range(2):
            part = pl.ds(n * 256 + half, 128, stride=2)
            total = raw[part, :] + blk[part, :]
            if n < 2:
                total = total + mer[part, :]
            if n < 1:
                total = total + ply[part, :]
            total = total.T
            if half == 0:
                tangent[0:128, place] = total
            else:
                tangent[128:243, place] = total[0:115]
                residual[:, place] = total[115:118] - load[:, place]
        results += started(
            [pltpu.make_async_copy(tangent.at[:, place], tangent_out.at[:, place], sems.at[5 + n])]
        )
    results += started([pltpu.make_async_copy(residual, residual_out.at[:, columns], sems.at[9])])
    done(results)


def scratch_of(table_size, slot_tiles, groups, acc_rows):
    f32, i32 = jnp.float32, jnp.int32
    return (
        [
            pltpu.VMEM((slot_tiles * 8, 128), i32),
            pltpu.VMEM((slot_tiles * 64, 128), i32),
            pltpu.VMEM((8 * 72, 128), f32),
            pltpu.VMEM((64, 128), f32),
            pltpu.VMEM((512, 128), f32),
            pltpu.VMEM((table_size, 128), f32),
            pltpu.VMEM((table_size, 384), jnp.bfloat16),
        ]
        + [pltpu.VMEM((8 * 24 * 8, 128), f32)] * 4
        + [pltpu.VMEM((8 * 6 * 8, 128), f32)]
        + [pltpu.VMEM((256, 128), f32)] * 4
        + [
            pltpu.VMEM((2 * TILES, 4, 128), i32),
            pltpu.VMEM((groups * VROWS, 128), f32),
            pltpu.VMEM((groups * 192, 128), f32),
            pltpu.SMEM((40,), i32),
            pltpu.SemaphoreType.DMA((5, 16)),
            pltpu.SemaphoreType.DMA((AHEAD + 1,)),
        ]
        + [pltpu.SMEM((4, 128), i32)] * (AHEAD + 1)
        + [pltpu.VMEM((acc_rows, 128), f32)] * WAYS
    )


def body(
    connectivity,
    slot_map,
    material_ids,
    element_counts,
    inverse_jacobians,
    quadrature_weights,
    materials,
    displacement,
    previous,
    load,
):
    f32, i32 = jnp.float32, jnp.int32
    state = lax.optimization_barrier(jnp.concatenate([displacement, previous], axis=0))
    shared = state[:, :512]
    ghost_blk = shifted(shared, "blk", -1)
    ghost_mer = shifted(shared, "mer", -1)
    ghost_ply = shifted(shared, "ply", -1)
    ids = material_ids.reshape(TILES, 128)
    connectivity, slot_map = tiles_first(connectivity), tiles_first(slot_map)
    inverse_jacobians, quadrature_weights = tiles_first(inverse_jacobians), tiles_first(quadrature_weights)
    anywhere = pl.BlockSpec(memory_space=pl.ANY)
    hbm = pl.BlockSpec(memory_space=pltpu.HBM)
    blocks, res, face_blk, face_mer, face_ply = pl.pallas_call(
        face_kernel,
        out_shape=[
            jax.ShapeDtypeStruct((VROWS, 128), f32),
            jax.ShapeDtypeStruct((192, 128), f32),
            jax.ShapeDtypeStruct((1024, 128), f32),
            jax.ShapeDtypeStruct((512, 128), f32),
            jax.ShapeDtypeStruct((256, 128), f32),
        ],
        in_specs=[hbm] * 4 + [anywhere] * 3 + [hbm] * 4,
        out_specs=[hbm] * 5,
        scratch_shapes=[
            pltpu.SMEM((1,), i32),
            pltpu.SMEM(materials.shape, f32),
            pltpu.VMEM((8, 128), i32),
            pltpu.VMEM((6, NODES), f32),
        ]
        + [pltpu.VMEM((6, 512), f32)] * 3
        + [pltpu.VMEM((rows, 128), f32) for rows in (1024, 512, 256)]
        + scratch_of(184, 8, 1, 1792),
        compiler_params=pltpu.CompilerParams(vmem_limit_bytes=VMEM),
        name="faces",
    )(
        element_counts, materials, ids, state, ghost_blk, ghost_mer, ghost_ply,
        connectivity, slot_map, inverse_jacobians, quadrature_weights,
    )
    back_ply = shifted(face_ply, "ply", 1)
    back_mer = shifted(face_mer, "mer", 1)
    back_blk = shifted(face_blk, "blk", 1)
    residual, tangent, raw = pl.pallas_call(
        own_kernel,
        out_shape=[
            jax.ShapeDtypeStruct((3, NODES), f32),
            jax.ShapeDtypeStruct((9 * SLOTS, NODES), f32),
            jax.ShapeDtypeStruct((1024, 128), f32),
        ],
        in_specs=[hbm] * 11,
        out_specs=[hbm] * 3,
        scratch_shapes=[
            pltpu.SMEM((1,), i32),
            pltpu.SMEM(materials.shape, f32),
            pltpu.VMEM((8, 128), i32),
            pltpu.VMEM((6, NODES), f32),
            pltpu.VMEM((3, NODES), f32),
            pltpu.VMEM((3, NODES), f32),
            pltpu.VMEM((9 * SLOTS, NODES), f32),
            pltpu.VMEM((1024, 128), f32),
        ]
        + scratch_of(128, 16, 2, 2 * NODES),
        compiler_params=pltpu.CompilerParams(vmem_limit_bytes=VMEM),
        cost_estimate=pl.CostEstimate(flops=10**8, bytes_accessed=10**8, transcendentals=0),
        name="own",
    )(
        element_counts, materials, ids, state, load,
        connectivity, slot_map, inverse_jacobians, quadrature_weights, blocks, res,
    )
    return pl.pallas_call(
        back_kernel,
        out_shape=[
            jax.ShapeDtypeStruct((3, NODES), f32),
            jax.ShapeDtypeStruct((9 * SLOTS, NODES), f32),
        ],
        in_specs=[hbm] * 3 + [anywhere] * 3 + [hbm],
        out_specs=[hbm] * 2,
        scratch_shapes=[
            pltpu.VMEM((1024, 128), f32),
            pltpu.VMEM((1024, 128), f32),
            pltpu.VMEM((512, 128), f32),
            pltpu.VMEM((256, 128), f32),
            pltpu.VMEM((3, 512), f32),
            pltpu.VMEM((3, 512), f32),
            pltpu.VMEM((9 * SLOTS, 512), f32),
            pltpu.SemaphoreType.DMA((10,)),
        ],
        input_output_aliases={0: 0, 1: 1},
        compiler_params=pltpu.CompilerParams(vmem_limit_bytes=8 * 1024 * 1024),
        name="back",
    )(residual, tangent, raw, back_blk, back_mer, back_ply, load)


def solution(mesh):
    return jax.shard_map(
        body,
        mesh=mesh,
        in_specs=(
            P(None, ("blk", "mer", "ply")),
            P(None, ("blk", "mer", "ply")),
            P(("blk", "mer", "ply")),
            P(("blk", "mer", "ply")),
            P(None, ("blk", "mer", "ply")),
            P(None, ("blk", "mer", "ply")),
            P(),
            P(None, ("blk", "mer", "ply")),
            P(None, ("blk", "mer", "ply")),
            P(None, ("blk", "mer", "ply")),
        ),
        out_specs=(P(None, ("blk", "mer", "ply")), P(None, ("blk", "mer", "ply"))),
        check_vma=False,
    )
```

```python
import math

import jax
import jax.numpy as jnp
from jax import lax
from jax.experimental import pallas as pl
from jax.experimental.pallas import tpu as pltpu
from jax.sharding import PartitionSpec as P

SLOTS = 27
NODES = 2048
ELEMS = 2048
TILES = 16
WAYS = 8
VROWS = 8 * 9 * 64
VMEM = 60 * 1024 * 1024
AHEAD = 3

SIGNS = [
    [-1, -1, -1],
    [1, -1, -1],
    [1, 1, -1],
    [-1, 1, -1],
    [-1, -1, 1],
    [1, -1, 1],
    [1, 1, 1],
    [-1, 1, 1],
]
OTHERS = [(1, 2), (0, 2), (0, 1)]
SYM = [(0, 0), (0, 1), (0, 2), (1, 1), (1, 2), (2, 2)]


def shifted(value, axis, steps):
    count = lax.axis_size(axis)
    pairs = [(source, (source + steps) % count) for source in range(count)]
    return lax.ppermute(value, axis, pairs)


def sym(i, j):
    return SYM.index((min(i, j), max(i, j)))


def shape_factors(q):
    bits = [(q ^ (q >> 1)) & 1, (q >> 1) & 1, q >> 2]
    plus, minus = 1.0 + 1.0 / math.sqrt(3.0), 1.0 - 1.0 / math.sqrt(3.0)
    table = {}
    for k in range(3):
        m, n = OTHERS[k]
        for sm in range(2):
            for sn in range(2):
                like = (bits[m] == sm).astype(jnp.int32) + (bits[n] == sn).astype(jnp.int32)
                table[k, sm, sn] = jnp.where(
                    like == 2, plus * plus / 8.0, jnp.where(like == 1, plus * minus / 8.0, minus * minus / 8.0)
                )
    return table


def tiles_first(x):
    rows, columns = x.shape
    x = x.reshape(rows // 8, 8, columns // 128, 128).transpose(0, 2, 1, 3)
    return x.reshape(rows * columns // 128, 128)


def half_copies(src, dst, group, count, sem):
    return [
        pltpu.make_async_copy(
            src.at[pl.ds(n * 128 + group * 64, 64), :], dst.at[pl.ds(n * 64, 64), :], sem.at[n]
        )
        for n in range(count)
    ]


def split_table(table, tparts):
    value = table[...]
    high = value.astype(jnp.bfloat16)
    rest = value - high.astype(jnp.float32)
    mid = rest.astype(jnp.bfloat16)
    low = (rest - mid.astype(jnp.float32)).astype(jnp.bfloat16)
    tparts[:, 0:128] = high
    tparts[:, 128:256] = mid
    tparts[:, 256:384] = low


def gather_nodal(conn, tparts, nodal):
    lanes = lax.broadcasted_iota(jnp.int32, (128, 128), 0)

    def step(t, carry):
        for half in range(2):
            blocks = 16 if half == 0 else tparts.shape[0] // 8
            rows = []
            hots = []
            for c in range(4):
                row = conn[pl.ds(t * 8 + half * 4 + c, 1), :]
                rows.append(jnp.broadcast_to(row >> 7, (8, 128)))
                hot = jnp.broadcast_to(row & 127, (128, 128)) == lanes
                hots.append(jnp.where(hot, 1.0, 0.0).astype(jnp.bfloat16))
            hot = jnp.concatenate(hots, axis=1)
            hot = jnp.concatenate([hot, hot, hot], axis=0)
            got = jnp.dot(tparts[0 : blocks * 8, :], hot, preferred_element_type=jnp.float32)
            for c in range(4):
                acc = got[0:8, c * 128 : (c + 1) * 128]
                for h in range(1, blocks):
                    piece = got[h * 8 : h * 8 + 8, c * 128 : (c + 1) * 128]
                    acc = jnp.where(rows[c] == h, piece, acc)
                nodal[pl.ds((half * 4 + c) * 64 + t, 8, stride=8), :] = acc
        return carry

    lax.fori_loop(0, 8, step, 0)


def point_stage(jac, weights, nodal, living, lame, shear, visc, grads, pushed, wsg, wpush, wleft, res):
    res[...] = jnp.zeros_like(res)

    def step(q, carry):
        base = q * 9
        w = jnp.where(living, weights[pl.ds(q, 8, stride=8), :], 0.0)
        jac_rows = []
        for k in range(3):
            rows = [base + 3 * k + l for l in range(3)]
            jac_rows.append([jac[pl.ds((row >> 3) * 64 + (row & 7), 8, stride=8), :] for row in rows])
        scaled = {
            (k, sm, sn): [jac_rows[k][l] * factor for l in range(3)]
            for (k, sm, sn), factor in shape_factors(q).items()
        }
        g = []
        for a in range(8):
            rows = []
            for l in range(3):
                total = None
                for k in range(3):
                    m, n = OTHERS[k]
                    term = scaled[k, (SIGNS[a][m] + 1) // 2, (SIGNS[a][n] + 1) // 2][l]
                    if total is None:
                        total = term if SIGNS[a][k] > 0 else -term
                    else:
                        total = total + term if SIGNS[a][k] > 0 else total - term
                rows.append(total)
            g.append(rows)
        for a in range(8):
            for l in range(3):
                grads[pl.ds(pl.multiple_of((q * 24 + a * 3 + l) * 8, 8), 8), :] = g[a][l]

        def gradient(first):
            rows = [[None] * 3 for _ in range(3)]
            for i in range(3):
                for a in range(8):
                    u = nodal[(a * 8 + first + i) * 8 : (a * 8 + first + i) * 8 + 8, :]
                    for l in range(3):
                        term = u * g[a][l]
                        rows[i][l] = term if a == 0 else rows[i][l] + term
                rows[i][i] = rows[i][i] + 1.0
            return rows

        def right(f):
            return [f[0][l] * f[0][m] + f[1][l] * f[1][m] + f[2][l] * f[2][m] for l, m in SYM]

        old = right(gradient(3))
        f = gradient(0)
        new = right(f)
        strain = [0.5 * (new[s] - (1.0 if l == m else 0.0)) for s, (l, m) in enumerate(SYM)]
        change = [0.5 * (new[s] - old[s]) for s in range(6)]
        trace = lame * (strain[0] + strain[3] + strain[5])
        mu2, visc2 = 2.0 * shear, 2.0 * visc
        stress = []
        for s, (l, m) in enumerate(SYM):
            value = mu2 * strain[s] + visc2 * change[s]
            stress.append(w * (value + trace if l == m else value))
        modulus = w * (shear + visc)
        for s, (i, j) in enumerate(SYM):
            left = f[i][0] * f[j][0] + f[i][1] * f[j][1] + f[i][2] * f[j][2]
            wleft[pl.ds(pl.multiple_of((q * 6 + s) * 8, 8), 8), :] = modulus * left
        for a in range(8):
            sg = [
                stress[sym(l, 0)] * g[a][0] + stress[sym(l, 1)] * g[a][1] + stress[sym(l, 2)] * g[a][2]
                for l in range(3)
            ]
            for i in range(3):
                start = pl.multiple_of((q * 24 + a * 3 + i) * 8, 8)
                value = f[i][0] * g[a][0] + f[i][1] * g[a][1] + f[i][2] * g[a][2]
                pushed[pl.ds(start, 8), :] = value
                wpush[pl.ds(start, 8), :] = w * value
                wsg[pl.ds(start, 8), :] = sg[i]
                term = f[i][0] * sg[0] + f[i][1] * sg[1] + f[i][2] * sg[2]
                res[pl.ds((a * 3 + i) * 8, 8), :] += term
        return carry

    lax.fori_loop(0, 8, step, 0)


def pair_stage(lame, modulus, grads, pushed, wsg, wpush, wleft, blocks, vbase):
    def rows_of(ref, q, corner, width=24):
        return [
            ref[pl.ds(pl.multiple_of((q * width + corner * 3 + l) * 8, 8), 8), :] for l in range(3)
        ]

    def outer(a, carry):
        def inner(b, carry):
            prod = [None] * 9
            stretch = [None] * 6
            geo = None
            for q in range(8):
                ga = rows_of(grads, q, a)
                gb = rows_of(grads, q, b)
                sb = rows_of(wsg, q, b)
                pa = rows_of(wpush, q, a)
                pb = rows_of(pushed, q, b)
                metric = ga[0] * gb[0] + ga[1] * gb[1] + ga[2] * gb[2]
                bend = ga[0] * sb[0] + ga[1] * sb[1] + ga[2] * sb[2]
                geo = bend if q == 0 else geo + bend
                for i in range(3):
                    for j in range(3):
                        term = pa[i] * pb[j]
                        prod[3 * i + j] = term if q == 0 else prod[3 * i + j] + term
                for s in range(6):
                    term = metric * wleft[pl.ds((q * 6 + s) * 8, 8), :]
                    stretch[s] = term if q == 0 else stretch[s] + term
            for i in range(3):
                for j in range(3):
                    value = lame * prod[3 * i + j] + modulus * prod[3 * j + i] + stretch[sym(i, j)]
                    if i == j:
                        value = value + geo
                    first = pl.multiple_of(vbase + (a * 9 + 3 * i + j) * 64 + b * 8, 8)
                    blocks[pl.ds(first, 8), :] = value
                    second = pl.multiple_of(vbase + (b * 9 + 3 * j + i) * 64 + a * 8, 8)
                    blocks[pl.ds(second, 8), :] = value
            return carry

        return lax.fori_loop(a, 8, inner, carry)

    lax.fori_loop(0, 8, outer, 0)


def merge_stage(slots, tiles, blocks):
    def step(a, carry):
        rows = [slots[pl.ds(a * tiles * 8 + b, 8, stride=8), :] for b in range(8)]

        def at(ij, b):
            return pl.ds(pl.multiple_of((a * 9 + ij) * 64 + b * 8, 8), 8)

        for early in range(7):
            sums = [blocks[at(ij, early), :] for ij in range(9)]
            for late in range(early + 1, 8):
                same = rows[early] == rows[late]
                for ij in range(9):
                    sums[ij] = sums[ij] + jnp.where(same, blocks[at(ij, late), :], 0.0)
            for ij in range(9):
                blocks[at(ij, early), :] = sums[ij]
        return carry

    lax.fori_loop(0, 8, step, 0)


def expand(corner, group, t, slots, blocks, res, spread):
    sbase = pl.multiple_of((corner * (slots.shape[0] // 64) + group * 8 + t) * 8, 8)
    vbase = group * VROWS + corner * 576 + t
    lines = lax.broadcasted_iota(jnp.int32, (8, 128), 0)
    none = jnp.full((8, 128), 8, jnp.int32)
    found = [none] * 4
    for b in range(7, -1, -1):
        away = jnp.broadcast_to(slots[pl.ds(sbase + b, 1), :], (8, 128)) - lines
        found = [jnp.where(away == 8 * k, b, found[k]) for k in range(4)]
    valid = [f < 8 for f in found]
    found = [f & 7 for f in found]
    for ij in range(9):
        value = blocks[pl.ds(vbase + ij * 64, 8, stride=8), :]
        for k in range(4):
            picked = jnp.take_along_axis(value, found[k], axis=0, mode="promise_in_bounds")
            spread[27 * ij + 8 * k : 27 * ij + 8 * k + 8, :] = jnp.where(valid[k], picked, 0.0)
    spread[243:246, :] = res[pl.ds(group * 192 + corner * 24 + t, 3, stride=8), :]


def turn(spread, turned):
    for half in range(2):
        turned[pl.ds(half, 128, stride=2), :] = spread[half * 128 : half * 128 + 128, :].T


def scatter(index, unit, turned, accs):
    for first in range(0, 128, WAYS):
        places = [pl.ds(index[unit, first + v], 2) for v in range(WAYS)]
        sums = [
            accs[v][places[v], :] + turned[2 * (first + v) : 2 * (first + v) + 2, :] for v in range(WAYS)
        ]
        for v in range(WAYS):
            accs[v][places[v], :] = sums[v]


def run_quads(quads, count, spread, turned, accs, rows, index, sems, slots, blocks, res, first_tile):
    def fetch(quad, buffer):
        return pltpu.make_async_copy(rows.at[quads[quad]], index[buffer], sems.at[buffer])

    first = pltpu.make_async_copy(rows.at[quads[0]], index[AHEAD], sems.at[AHEAD])
    first.start()
    for n in range(AHEAD):
        fetch(n, n).start()
    for ref in spread:
        ref[...] = jnp.zeros_like(ref)
    turned[0][...] = jnp.zeros_like(turned[0])
    first.wait()

    def step(quad, carry):
        code = quads[quad]
        tile, corner = code >> 1, (code & 1) * 4
        group, t = (tile - first_tile) >> 3, tile & 7

        def work(now):
            before = (now - 1) % (AHEAD + 1)
            fetch(quad, now).wait()
            for n in range(4):
                expand(corner + n, group, t, slots, blocks, res, spread[n % 2])
                turn(spread[(n + 1) % 2], turned[(n + 1) % 2])
                if n < 2:
                    scatter(index[before], n + 2, turned[n % 2], accs)
                else:
                    scatter(index[now], n - 2, turned[n % 2], accs)

            @pl.when(quad + AHEAD < count)
            def _():
                fetch(quad + AHEAD, before).start()

        for now in range(AHEAD + 1):
            pl.when(lax.rem(quad, AHEAD + 1) == now)(lambda now=now: work(now))
        return carry

    lax.fori_loop(0, count, step, 0)
    turn(spread[1], turned[1])
    for now in range(AHEAD + 1):

        @pl.when(lax.rem(count - 1, AHEAD + 1) == now)
        def _(now=now):
            scatter(index[now], 2, turned[0], accs)
            scatter(index[now], 3, turned[1], accs)


def materials_of(ids, materials):
    params = []
    for row in range(3):
        value = jnp.zeros((8, 128), jnp.float32)
        for m in range(8):
            value = jnp.where(ids == m, materials[row, m], value)
        params.append(value)
    return params


def zero(refs):
    for ref in refs:
        rows = ref.shape[0]

        def step(i, carry, ref=ref):
            ref[pl.ds(pl.multiple_of(i * 256, 256), 256), :] = jnp.zeros((256, 128), jnp.float32)
            return carry

        lax.fori_loop(0, rows // 256, step, 0)


def table_rows(table, state, blocks, first):
    for h in range(blocks):
        start = (first + h) * 8
        table[start : start + 6, :] = state[0:6, h * 128 : h * 128 + 128]


def scatter_rows(conn, rows, tiles, first_tile):
    for tile in range(tiles):
        for half in range(2):
            node = conn[tile * 8 + half * 4 : tile * 8 + half * 4 + 4, :]
            node = jnp.where(node >= NODES, node - NODES, node)
            rows[(first_tile + tile) * 2 + half] = node * 2


def started(copies):
    for copy in copies:
        copy.start()
    return copies


def done(copies):
    for copy in copies:
        copy.wait()


def face_kernel(
    materials_hbm, ids_hbm, state_hbm, blk_hbm, mer_hbm, ply_hbm,
    conn_hbm, slot_hbm, jac_hbm, weight_hbm,
    blocks_out, res_out, out_blk, out_mer, out_ply,
    materials, ids, state, ghost_blk, ghost_mer, ghost_ply, sum_blk, sum_mer, sum_ply,
    conn, slots, jac, weights, nodal, table, tparts, grads, pushed, wsg, wpush, wleft,
    spread0, spread1, turned0, turned1, rows, blocks, res, quads, sems, index_sems, *more,
):
    index, accs = more[: AHEAD + 1], more[AHEAD + 1 :]
    nodes = started(
        [
            pltpu.make_async_copy(src, dst, sems.at[4, n])
            for n, (src, dst) in enumerate(
                [(state_hbm, state), (blk_hbm, ghost_blk), (mer_hbm, ghost_mer), (ply_hbm, ghost_ply)]
            )
        ]
        + half_copies(conn_hbm, conn, 1, 1, sems.at[0])
    )
    points = started(
        [
            pltpu.make_async_copy(ids_hbm.at[pl.ds(8, 8), :], ids, sems.at[4, 4]),
            pltpu.make_async_copy(materials_hbm, materials, sems.at[4, 8]),
        ]
        + half_copies(weight_hbm, weights, 1, 1, sems.at[1])
        + half_copies(jac_hbm, jac, 1, 9, sems.at[2])
    )
    pairs = started(half_copies(slot_hbm, slots, 1, 8, sems.at[3]))
    table[...] = jnp.zeros_like(table)
    zero(accs)
    done(nodes)
    table_rows(table, state, 16, 0)
    table_rows(table, ghost_blk, 4, 16)
    table_rows(table, ghost_mer, 2, 20)
    table_rows(table, ghost_ply, 1, 22)
    split_table(table, tparts)
    scatter_rows(conn, rows, 8, 8)
    gather_nodal(conn, tparts, nodal)
    done(points)
    lame, shear, visc = materials_of(ids[...], materials)
    tile = lax.broadcasted_iota(jnp.int32, (8, 128), 0)
    lane = lax.broadcasted_iota(jnp.int32, (8, 128), 1)
    used = jnp.broadcast_to(state[6:7, 0:128], (8, 128)).astype(jnp.int32)
    living = (tile > 0) | (lane + 1024 < used)
    point_stage(jac, weights, nodal, living, lame, shear, visc, grads, pushed, wsg, wpush, wleft, res)
    pair_stage(lame, shear + visc, grads, pushed, wsg, wpush, wleft, blocks, 0)
    done(pairs)
    merge_stage(slots, 8, blocks)
    results = started(
        [
            pltpu.make_async_copy(blocks, blocks_out, sems.at[4, 5]),
            pltpu.make_async_copy(res, res_out, sems.at[4, 6]),
        ]
    )
    mer = (lax.axis_index("mer") < lax.axis_size("mer") - 1).astype(jnp.int32)
    ply = (lax.axis_index("ply") < lax.axis_size("ply") - 1).astype(jnp.int32)
    for n in range(4):
        quads[n] = (12 + n) * 2 + 1
    for n in range(2):
        quads[4 + n] = (10 + n) * 2 + 1
    quads[4 + 2 * mer] = 9 * 2 + 1
    count = 4 + 2 * mer + ply
    run_quads(
        quads, count, (spread0, spread1), (turned0, turned1), accs, rows, index, index_sems,
        slots, blocks, res, 8,
    )
    first = 0
    for n, (part, out) in enumerate([(sum_blk, out_blk), (sum_mer, out_mer), (sum_ply, out_ply)]):
        size = part.shape[0]
        total = accs[0][first : first + size, :]
        for acc in accs[1:]:
            total = total + acc[first : first + size, :]
        part[...] = total
        results += started([pltpu.make_async_copy(part, out, sems.at[4, 9 + n])])
        first += size
    done(results)


def own_kernel(
    materials_hbm, ids_hbm, state_hbm, load_hbm,
    conn_hbm, slot_hbm, jac_hbm, weight_hbm, blocks_hbm, res_hbm,
    residual_out, tangent_out,
    materials, ids, state, load, residual, tangent,
    conn, slots, jac, weights, nodal, table, tparts, grads, pushed, wsg, wpush, wleft,
    spread0, spread1, turned0, turned1, rows, blocks, res, quads, sems, index_sems, *more,
):
    index, accs = more[: AHEAD + 1], more[AHEAD + 1 :]
    nodes = started(
        [pltpu.make_async_copy(state_hbm, state, sems.at[4, 0])]
        + [pltpu.make_async_copy(conn_hbm, conn, sems.at[0, 0])]
    )
    points = started(
        [
            pltpu.make_async_copy(ids_hbm.at[pl.ds(0, 8), :], ids, sems.at[4, 1]),
            pltpu.make_async_copy(materials_hbm, materials, sems.at[4, 13]),
        ]
        + half_copies(weight_hbm, weights, 0, 1, sems.at[1])
        + half_copies(jac_hbm, jac, 0, 9, sems.at[2])
    )
    pairs = started([pltpu.make_async_copy(slot_hbm, slots, sems.at[3, 0])])
    units = started(
        [
            pltpu.make_async_copy(blocks_hbm, blocks.at[pl.ds(VROWS, VROWS), :], sems.at[4, 2]),
            pltpu.make_async_copy(res_hbm, res.at[pl.ds(192, 192), :], sems.at[4, 3]),
            pltpu.make_async_copy(load_hbm, load, sems.at[4, 4]),
        ]
    )
    table[...] = jnp.zeros_like(table)
    zero(accs)
    done(nodes)
    table_rows(table, state, 16, 0)
    split_table(table, tparts)
    scatter_rows(conn, rows, 16, 0)
    gather_nodal(conn, tparts, nodal)
    done(points)
    lame, shear, visc = materials_of(ids[...], materials)
    tile = lax.broadcasted_iota(jnp.int32, (8, 128), 0)
    lane = lax.broadcasted_iota(jnp.int32, (8, 128), 1)
    used = jnp.broadcast_to(state[6:7, 0:128], (8, 128)).astype(jnp.int32)
    living = tile * 128 + lane < used
    point_stage(
        jac, weights, nodal, living, lame, shear, visc, grads, pushed, wsg, wpush, wleft,
        res.at[pl.ds(0, 192), :],
    )
    pair_stage(lame, shear + visc, grads, pushed, wsg, wpush, wleft, blocks, 0)
    done(pairs)
    merge_stage(slots, 16, blocks)
    done(units)

    def put(tile, halves, count):
        for n, half in enumerate(halves):
            quads[count + n] = tile * 2 + half
        return count + len(halves)

    has_mer = lax.axis_index("mer") < lax.axis_size("mer") - 1
    has_ply = lax.axis_index("ply") < lax.axis_size("ply") - 1
    count = 0
    for tile in range(9, 16):
        count = put(tile, (0,), count)
    count = lax.fori_loop(0, (state[6, 0].astype(jnp.int32) + 127) // 128, lambda tile, n: put(tile, (0, 1), n), count)
    count = lax.fori_loop(9, jnp.where(has_ply, 9, 10), lambda tile, n: put(tile, (1,), n), count)
    count = lax.fori_loop(10, jnp.where(has_mer, 10, 12), lambda tile, n: put(tile, (1,), n), count)
    run_quads(
        quads, count, (spread0, spread1), (turned0, turned1), accs, rows, index, index_sems,
        slots, blocks, res, 0,
    )

    def add_up(part):
        total = accs[0][part, :]
        for acc in accs[1:]:
            total = total + acc[part, :]
        return total

    results = []

    def finish(step, carry):
        for k in range(2):
            n = step * 2 + k
            columns = pl.ds(pl.multiple_of(n * 128, 128), 128)
            tangent[0:128, columns] = add_up(pl.ds(n * 256, 128, stride=2)).T
            total = add_up(pl.ds(n * 256 + 1, 128, stride=2)).T
            tangent[128:243, columns] = total[0:115]
            residual[:, columns] = total[115:118] - load[:, columns]
        return carry

    for part in range(4):
        lax.fori_loop(part * 2, part * 2 + 2, finish, 0)
        columns = pl.ds(part * 512, 512)
        results += started(
            [
                pltpu.make_async_copy(tangent.at[:, columns], tangent_out.at[:, columns], sems.at[4, 5 + part]),
                pltpu.make_async_copy(residual.at[:, columns], residual_out.at[:, columns], sems.at[4, 9 + part]),
            ]
        )
    done(results)


def back_kernel(
    residual_in, tangent_in, blk_hbm, mer_hbm, ply_hbm, residual_out, tangent_out,
    blk, mer, ply, residual, tangent, sems,
):
    columns = pl.ds(0, 512)
    done(
        started(
            [
                pltpu.make_async_copy(src, dst, sems.at[n])
                for n, (src, dst) in enumerate(
                    [
                        (blk_hbm, blk),
                        (mer_hbm, mer),
                        (ply_hbm, ply),
                        (residual_in.at[:, columns], residual),
                        (tangent_in.at[:, columns], tangent),
                    ]
                )
            ]
        )
    )
    results = []
    for n in range(4):
        place = pl.ds(n * 128, 128)
        for half in range(2):
            part = pl.ds(n * 256 + half, 128, stride=2)
            total = blk[part, :]
            if n < 2:
                total = total + mer[part, :]
            if n < 1:
                total = total + ply[part, :]
            total = total.T
            if half == 0:
                tangent[0:128, place] += total
            else:
                tangent[128:243, place] += total[0:115]
                residual[:, place] += total[115:118]
        results += started(
            [pltpu.make_async_copy(tangent.at[:, place], tangent_out.at[:, place], sems.at[5 + n])]
        )
    results += started([pltpu.make_async_copy(residual, residual_out.at[:, columns], sems.at[9])])
    done(results)


def scratch_of(table_size, slot_tiles, groups, acc_rows):
    f32, i32 = jnp.float32, jnp.int32
    return (
        [
            pltpu.VMEM((slot_tiles * 8, 128), i32),
            pltpu.VMEM((slot_tiles * 64, 128), i32),
            pltpu.VMEM((8 * 72, 128), f32),
            pltpu.VMEM((64, 128), f32),
            pltpu.VMEM((512, 128), f32),
            pltpu.VMEM((table_size, 128), f32),
            pltpu.VMEM((table_size, 384), jnp.bfloat16),
        ]
        + [pltpu.VMEM((8 * 24 * 8, 128), f32)] * 4
        + [pltpu.VMEM((8 * 6 * 8, 128), f32)]
        + [pltpu.VMEM((256, 128), f32)] * 4
        + [
            pltpu.VMEM((2 * TILES, 4, 128), i32),
            pltpu.VMEM((groups * VROWS, 128), f32),
            pltpu.VMEM((groups * 192, 128), f32),
            pltpu.SMEM((40,), i32),
            pltpu.SemaphoreType.DMA((5, 16)),
            pltpu.SemaphoreType.DMA((AHEAD + 1,)),
        ]
        + [pltpu.SMEM((4, 128), i32)] * (AHEAD + 1)
        + [pltpu.VMEM((acc_rows, 128), f32)] * WAYS
    )


def body(
    connectivity,
    slot_map,
    material_ids,
    element_counts,
    inverse_jacobians,
    quadrature_weights,
    materials,
    displacement,
    previous,
    load,
):
    f32, i32 = jnp.float32, jnp.int32
    count = jnp.broadcast_to(element_counts.astype(f32)[:, None], (1, NODES))
    state = lax.optimization_barrier(jnp.concatenate([displacement, previous, count], axis=0))
    ghost_blk = shifted(state[:6, :512], "blk", -1)
    ghost_mer = shifted(state[:6, :256], "mer", -1)
    ghost_ply = shifted(state[:6, :128], "ply", -1)
    ids = material_ids.reshape(TILES, 128)
    connectivity, slot_map = tiles_first(connectivity), tiles_first(slot_map)
    inverse_jacobians, quadrature_weights = tiles_first(inverse_jacobians), tiles_first(quadrature_weights)
    anywhere = pl.BlockSpec(memory_space=pl.ANY)
    hbm = pl.BlockSpec(memory_space=pltpu.HBM)
    blocks, res, face_blk, face_mer, face_ply = pl.pallas_call(
        face_kernel,
        out_shape=[
            jax.ShapeDtypeStruct((VROWS, 128), f32),
            jax.ShapeDtypeStruct((192, 128), f32),
            jax.ShapeDtypeStruct((1024, 128), f32),
            jax.ShapeDtypeStruct((512, 128), f32),
            jax.ShapeDtypeStruct((256, 128), f32),
        ],
        in_specs=[hbm] * 3 + [anywhere] * 3 + [hbm] * 4,
        out_specs=[hbm] * 5,
        scratch_shapes=[
            pltpu.SMEM(materials.shape, f32),
            pltpu.VMEM((8, 128), i32),
            pltpu.VMEM((7, NODES), f32),
        ]
        + [pltpu.VMEM((6, columns), f32) for columns in (512, 256, 128)]
        + [pltpu.VMEM((rows, 128), f32) for rows in (1024, 512, 256)]
        + scratch_of(192, 8, 1, 1792),
        compiler_params=pltpu.CompilerParams(vmem_limit_bytes=VMEM),
        name="faces",
    )(
        materials, ids, state, ghost_blk, ghost_mer, ghost_ply,
        connectivity, slot_map, inverse_jacobians, quadrature_weights,
    )
    back_ply = shifted(face_ply, "ply", 1)
    back_mer = shifted(face_mer, "mer", 1)
    back_blk = shifted(face_blk, "blk", 1)
    residual, tangent = pl.pallas_call(
        own_kernel,
        out_shape=[
            jax.ShapeDtypeStruct((3, NODES), f32),
            jax.ShapeDtypeStruct((9 * SLOTS, NODES), f32),
        ],
        in_specs=[hbm] * 10,
        out_specs=[hbm] * 2,
        scratch_shapes=[
            pltpu.SMEM(materials.shape, f32),
            pltpu.VMEM((8, 128), i32),
            pltpu.VMEM((7, NODES), f32),
            pltpu.VMEM((3, NODES), f32),
            pltpu.VMEM((3, NODES), f32),
            pltpu.VMEM((9 * SLOTS, NODES), f32),
        ]
        + scratch_of(128, 16, 2, 2 * NODES),
        compiler_params=pltpu.CompilerParams(vmem_limit_bytes=VMEM),
        cost_estimate=pl.CostEstimate(flops=10**8, bytes_accessed=10**8, transcendentals=0),
        name="own",
    )(
        materials, ids, state, load,
        connectivity, slot_map, inverse_jacobians, quadrature_weights, blocks, res,
    )
    return pl.pallas_call(
        back_kernel,
        out_shape=[
            jax.ShapeDtypeStruct((3, NODES), f32),
            jax.ShapeDtypeStruct((9 * SLOTS, NODES), f32),
        ],
        in_specs=[hbm] * 2 + [anywhere] * 3,
        out_specs=[hbm] * 2,
        scratch_shapes=[
            pltpu.VMEM((1024, 128), f32),
            pltpu.VMEM((512, 128), f32),
            pltpu.VMEM((256, 128), f32),
            pltpu.VMEM((3, 512), f32),
            pltpu.VMEM((9 * SLOTS, 512), f32),
            pltpu.SemaphoreType.DMA((10,)),
        ],
        input_output_aliases={0: 0, 1: 1},
        compiler_params=pltpu.CompilerParams(vmem_limit_bytes=8 * 1024 * 1024),
        name="back",
    )(residual, tangent, back_blk, back_mer, back_ply)


def solution(mesh):
    return jax.shard_map(
        body,
        mesh=mesh,
        in_specs=(
            P(None, ("blk", "mer", "ply")),
            P(None, ("blk", "mer", "ply")),
            P(("blk", "mer", "ply")),
            P(("blk", "mer", "ply")),
            P(None, ("blk", "mer", "ply")),
            P(None, ("blk", "mer", "ply")),
            P(),
            P(None, ("blk", "mer", "ply")),
            P(None, ("blk", "mer", "ply")),
            P(None, ("blk", "mer", "ply")),
        ),
        out_specs=(P(None, ("blk", "mer", "ply")), P(None, ("blk", "mer", "ply"))),
        check_vma=False,
    )
```

```python
import math

import jax
import jax.numpy as jnp
from jax import lax
from jax.experimental import pallas as pl
from jax.experimental.pallas import tpu as pltpu
from jax.sharding import PartitionSpec as P

SLOTS = 27
NODES = 2048
ELEMS = 2048
TILES = 16
WAYS = 8
VROWS = 8 * 9 * 64
VMEM = 60 * 1024 * 1024
AHEAD = 3

SIGNS = [
    [-1, -1, -1],
    [1, -1, -1],
    [1, 1, -1],
    [-1, 1, -1],
    [-1, -1, 1],
    [1, -1, 1],
    [1, 1, 1],
    [-1, 1, 1],
]
OTHERS = [(1, 2), (0, 2), (0, 1)]
SYM = [(0, 0), (0, 1), (0, 2), (1, 1), (1, 2), (2, 2)]


def shifted(value, axis, steps):
    count = lax.axis_size(axis)
    pairs = [(source, (source + steps) % count) for source in range(count)]
    return lax.ppermute(value, axis, pairs)


def sym(i, j):
    return SYM.index((min(i, j), max(i, j)))


def shape_factors(q):
    bits = [(q ^ (q >> 1)) & 1, (q >> 1) & 1, q >> 2]
    plus, minus = 1.0 + 1.0 / math.sqrt(3.0), 1.0 - 1.0 / math.sqrt(3.0)
    table = {}
    for k in range(3):
        m, n = OTHERS[k]
        for sm in range(2):
            for sn in range(2):
                like = (bits[m] == sm).astype(jnp.int32) + (bits[n] == sn).astype(jnp.int32)
                table[k, sm, sn] = jnp.where(
                    like == 2, plus * plus / 8.0, jnp.where(like == 1, plus * minus / 8.0, minus * minus / 8.0)
                )
    return table


def tiles_first(x):
    rows, columns = x.shape
    x = x.reshape(rows // 8, 8, columns // 128, 128).transpose(0, 2, 1, 3)
    return x.reshape(rows * columns // 128, 128)


def half_copies(src, dst, group, count, sem):
    return [
        pltpu.make_async_copy(
            src.at[pl.ds(n * 128 + group * 64, 64), :], dst.at[pl.ds(n * 64, 64), :], sem.at[n]
        )
        for n in range(count)
    ]


def split_table(table, tparts):
    value = table[...]
    high = value.astype(jnp.bfloat16)
    rest = value - high.astype(jnp.float32)
    mid = rest.astype(jnp.bfloat16)
    low = (rest - mid.astype(jnp.float32)).astype(jnp.bfloat16)
    tparts[:, 0:128] = high
    tparts[:, 128:256] = mid
    tparts[:, 256:384] = low


def gather_nodal(conn, tparts, nodal):
    lanes = lax.broadcasted_iota(jnp.int32, (128, 128), 0)

    def step(t, carry):
        for half in range(2):
            blocks = 16 if half == 0 else tparts.shape[0] // 8
            rows = []
            hots = []
            for c in range(4):
                row = conn[pl.ds(t * 8 + half * 4 + c, 1), :]
                rows.append(jnp.broadcast_to(row >> 7, (8, 128)))
                hot = jnp.broadcast_to(row & 127, (128, 128)) == lanes
                hots.append(jnp.where(hot, 1.0, 0.0).astype(jnp.bfloat16))
            hot = jnp.concatenate(hots, axis=1)
            hot = jnp.concatenate([hot, hot, hot], axis=0)
            got = jnp.dot(tparts[0 : blocks * 8, :], hot, preferred_element_type=jnp.float32)
            for c in range(4):
                acc = got[0:8, c * 128 : (c + 1) * 128]
                for h in range(1, blocks):
                    piece = got[h * 8 : h * 8 + 8, c * 128 : (c + 1) * 128]
                    acc = jnp.where(rows[c] == h, piece, acc)
                nodal[pl.ds((half * 4 + c) * 64 + t, 8, stride=8), :] = acc
        return carry

    lax.fori_loop(0, 8, step, 0)


def point_stage(jac, weights, nodal, living, lame, shear, visc, grads, pushed, wsg, wpush, wleft, res):
    res[...] = jnp.zeros_like(res)

    def step(q, carry):
        base = q * 9
        w = jnp.where(living, weights[pl.ds(q, 8, stride=8), :], 0.0)
        jac_rows = []
        for k in range(3):
            rows = [base + 3 * k + l for l in range(3)]
            jac_rows.append([jac[pl.ds((row >> 3) * 64 + (row & 7), 8, stride=8), :] for row in rows])
        scaled = {
            (k, sm, sn): [jac_rows[k][l] * factor for l in range(3)]
            for (k, sm, sn), factor in shape_factors(q).items()
        }
        g = []
        for a in range(8):
            rows = []
            for l in range(3):
                total = None
                for k in range(3):
                    m, n = OTHERS[k]
                    term = scaled[k, (SIGNS[a][m] + 1) // 2, (SIGNS[a][n] + 1) // 2][l]
                    if total is None:
                        total = term if SIGNS[a][k] > 0 else -term
                    else:
                        total = total + term if SIGNS[a][k] > 0 else total - term
                rows.append(total)
            g.append(rows)
        for a in range(8):
            for l in range(3):
                grads[pl.ds(pl.multiple_of((q * 24 + a * 3 + l) * 8, 8), 8), :] = g[a][l]

        def gradient(first):
            rows = [[None] * 3 for _ in range(3)]
            for i in range(3):
                for a in range(8):
                    u = nodal[(a * 8 + first + i) * 8 : (a * 8 + first + i) * 8 + 8, :]
                    for l in range(3):
                        term = u * g[a][l]
                        rows[i][l] = term if a == 0 else rows[i][l] + term
                rows[i][i] = rows[i][i] + 1.0
            return rows

        def right(f):
            return [f[0][l] * f[0][m] + f[1][l] * f[1][m] + f[2][l] * f[2][m] for l, m in SYM]

        old = right(gradient(3))
        f = gradient(0)
        new = right(f)
        strain = [0.5 * (new[s] - (1.0 if l == m else 0.0)) for s, (l, m) in enumerate(SYM)]
        change = [0.5 * (new[s] - old[s]) for s in range(6)]
        trace = lame * (strain[0] + strain[3] + strain[5])
        mu2, visc2 = 2.0 * shear, 2.0 * visc
        stress = []
        for s, (l, m) in enumerate(SYM):
            value = mu2 * strain[s] + visc2 * change[s]
            stress.append(w * (value + trace if l == m else value))
        modulus = w * (shear + visc)
        for s, (i, j) in enumerate(SYM):
            left = f[i][0] * f[j][0] + f[i][1] * f[j][1] + f[i][2] * f[j][2]
            wleft[pl.ds(pl.multiple_of((q * 6 + s) * 8, 8), 8), :] = modulus * left
        for a in range(8):
            sg = [
                stress[sym(l, 0)] * g[a][0] + stress[sym(l, 1)] * g[a][1] + stress[sym(l, 2)] * g[a][2]
                for l in range(3)
            ]
            for i in range(3):
                start = pl.multiple_of((q * 24 + a * 3 + i) * 8, 8)
                value = f[i][0] * g[a][0] + f[i][1] * g[a][1] + f[i][2] * g[a][2]
                pushed[pl.ds(start, 8), :] = value
                wpush[pl.ds(start, 8), :] = w * value
                wsg[pl.ds(start, 8), :] = sg[i]
                term = f[i][0] * sg[0] + f[i][1] * sg[1] + f[i][2] * sg[2]
                res[pl.ds((a * 3 + i) * 8, 8), :] += term
        return carry

    lax.fori_loop(0, 8, step, 0)


def pair_stage(lame, modulus, grads, pushed, wsg, wpush, wleft, blocks, vbase):
    def rows_of(ref, q, corner, width=24):
        return [
            ref[pl.ds(pl.multiple_of((q * width + corner * 3 + l) * 8, 8), 8), :] for l in range(3)
        ]

    def outer(a, carry):
        def inner(b, carry):
            prod = [None] * 9
            stretch = [None] * 6
            geo = None
            for q in range(8):
                ga = rows_of(grads, q, a)
                gb = rows_of(grads, q, b)
                sb = rows_of(wsg, q, b)
                pa = rows_of(wpush, q, a)
                pb = rows_of(pushed, q, b)
                metric = ga[0] * gb[0] + ga[1] * gb[1] + ga[2] * gb[2]
                bend = ga[0] * sb[0] + ga[1] * sb[1] + ga[2] * sb[2]
                geo = bend if q == 0 else geo + bend
                for i in range(3):
                    for j in range(3):
                        term = pa[i] * pb[j]
                        prod[3 * i + j] = term if q == 0 else prod[3 * i + j] + term
                for s in range(6):
                    term = metric * wleft[pl.ds((q * 6 + s) * 8, 8), :]
                    stretch[s] = term if q == 0 else stretch[s] + term
            for i in range(3):
                for j in range(3):
                    value = lame * prod[3 * i + j] + modulus * prod[3 * j + i] + stretch[sym(i, j)]
                    if i == j:
                        value = value + geo
                    first = pl.multiple_of(vbase + (a * 9 + 3 * i + j) * 64 + b * 8, 8)
                    blocks[pl.ds(first, 8), :] = value
                    second = pl.multiple_of(vbase + (b * 9 + 3 * j + i) * 64 + a * 8, 8)
                    blocks[pl.ds(second, 8), :] = value
            return carry

        return lax.fori_loop(a, 8, inner, carry)

    lax.fori_loop(0, 8, outer, 0)


def merge_stage(slots, tiles, blocks):
    def step(a, carry):
        rows = [slots[pl.ds(a * tiles * 8 + b, 8, stride=8), :] for b in range(8)]

        def at(ij, b):
            return pl.ds(pl.multiple_of((a * 9 + ij) * 64 + b * 8, 8), 8)

        for early in range(7):
            sums = [blocks[at(ij, early), :] for ij in range(9)]
            for late in range(early + 1, 8):
                same = rows[early] == rows[late]
                for ij in range(9):
                    sums[ij] = sums[ij] + jnp.where(same, blocks[at(ij, late), :], 0.0)
            for ij in range(9):
                blocks[at(ij, early), :] = sums[ij]
        return carry

    lax.fori_loop(0, 8, step, 0)


def expand(corner, group, t, slots, blocks, res, spread):
    sbase = pl.multiple_of((corner * (slots.shape[0] // 64) + group * 8 + t) * 8, 8)
    vbase = group * VROWS + corner * 576 + t
    lines = lax.broadcasted_iota(jnp.int32, (8, 128), 0)
    none = jnp.full((8, 128), 8, jnp.int32)
    found = [none] * 4
    for b in range(7, -1, -1):
        away = jnp.broadcast_to(slots[pl.ds(sbase + b, 1), :], (8, 128)) - lines
        found = [jnp.where(away == 8 * k, b, found[k]) for k in range(4)]
    valid = [f < 8 for f in found]
    found = [f & 7 for f in found]
    for ij in range(9):
        value = blocks[pl.ds(vbase + ij * 64, 8, stride=8), :]
        for k in range(4):
            picked = jnp.take_along_axis(value, found[k], axis=0, mode="promise_in_bounds")
            spread[27 * ij + 8 * k : 27 * ij + 8 * k + 8, :] = jnp.where(valid[k], picked, 0.0)
    spread[243:246, :] = res[pl.ds(group * 192 + corner * 24 + t, 3, stride=8), :]


def turn(spread, turned):
    for half in range(2):
        turned[pl.ds(half, 128, stride=2), :] = spread[half * 128 : half * 128 + 128, :].T


def scatter(index, unit, turned, accs):
    for first in range(0, 128, WAYS):
        places = [pl.ds(index[unit, first + v], 2) for v in range(WAYS)]
        sums = [
            accs[v][places[v], :] + turned[2 * (first + v) : 2 * (first + v) + 2, :] for v in range(WAYS)
        ]
        for v in range(WAYS):
            accs[v][places[v], :] = sums[v]


def run_quads(quads, count, spread, turned, accs, rows, index, sems, slots, blocks, res, first_tile):
    def fetch(quad, buffer):
        return pltpu.make_async_copy(rows.at[quads[quad]], index[buffer], sems.at[buffer])

    first = pltpu.make_async_copy(rows.at[quads[0]], index[AHEAD], sems.at[AHEAD])
    first.start()
    for n in range(AHEAD):
        fetch(n, n).start()
    for ref in spread:
        ref[...] = jnp.zeros_like(ref)
    turned[0][...] = jnp.zeros_like(turned[0])
    first.wait()

    def step(quad, carry):
        code = quads[quad]
        tile, corner = code >> 1, (code & 1) * 4
        group, t = (tile - first_tile) >> 3, tile & 7

        def work(now):
            before = (now - 1) % (AHEAD + 1)
            fetch(quad, now).wait()
            for n in range(4):
                expand(corner + n, group, t, slots, blocks, res, spread[n % 2])
                turn(spread[(n + 1) % 2], turned[(n + 1) % 2])
                if n < 2:
                    scatter(index[before], n + 2, turned[n % 2], accs)
                else:
                    scatter(index[now], n - 2, turned[n % 2], accs)

            @pl.when(quad + AHEAD < count)
            def _():
                fetch(quad + AHEAD, before).start()

        for now in range(AHEAD + 1):
            pl.when(lax.rem(quad, AHEAD + 1) == now)(lambda now=now: work(now))
        return carry

    lax.fori_loop(0, count, step, 0)
    turn(spread[1], turned[1])
    for now in range(AHEAD + 1):

        @pl.when(lax.rem(count - 1, AHEAD + 1) == now)
        def _(now=now):
            scatter(index[now], 2, turned[0], accs)
            scatter(index[now], 3, turned[1], accs)


def materials_of(ids, materials):
    params = []
    for row in range(3):
        value = jnp.zeros((8, 128), jnp.float32)
        for m in range(8):
            value = jnp.where(ids == m, materials[row, m], value)
        params.append(value)
    return params


def zero(refs):
    for ref in refs:
        rows = ref.shape[0]

        def step(i, carry, ref=ref):
            ref[pl.ds(pl.multiple_of(i * 256, 256), 256), :] = jnp.zeros((256, 128), jnp.float32)
            return carry

        lax.fori_loop(0, rows // 256, step, 0)


def table_rows(table, state, blocks, first):
    for h in range(blocks):
        start = (first + h) * 8
        table[start : start + 6, :] = state[0:6, h * 128 : h * 128 + 128]


def scatter_rows(conn, rows, tiles, first_tile):
    for tile in range(tiles):
        for half in range(2):
            node = conn[tile * 8 + half * 4 : tile * 8 + half * 4 + 4, :]
            node = jnp.where(node >= NODES, node - NODES, node)
            rows[(first_tile + tile) * 2 + half] = node * 2


def started(copies):
    for copy in copies:
        copy.start()
    return copies


def done(copies):
    for copy in copies:
        copy.wait()


def face_kernel(
    materials_hbm, ids_hbm, state_hbm, blk_hbm, mer_hbm, ply_hbm,
    conn_hbm, slot_hbm, jac_hbm, weight_hbm,
    blocks_out, res_out, out_blk, out_mer, out_ply,
    materials, ids, state, ghost_blk, ghost_mer, ghost_ply, sum_blk, sum_mer, sum_ply,
    conn, slots, jac, weights, nodal, table, tparts, grads, pushed, wsg, wpush, wleft,
    spread0, spread1, turned0, turned1, rows, blocks, res, quads, sems, index_sems, *more,
):
    index, accs = more[: AHEAD + 1], more[AHEAD + 1 :]
    nodes = started(
        [
            pltpu.make_async_copy(src, dst, sems.at[4, n])
            for n, (src, dst) in enumerate(
                [(state_hbm, state), (blk_hbm, ghost_blk), (mer_hbm, ghost_mer), (ply_hbm, ghost_ply)]
            )
        ]
        + half_copies(conn_hbm, conn, 1, 1, sems.at[0])
    )
    points = started(
        [
            pltpu.make_async_copy(ids_hbm.at[pl.ds(8, 8), :], ids, sems.at[4, 4]),
            pltpu.make_async_copy(materials_hbm, materials, sems.at[4, 8]),
        ]
        + half_copies(weight_hbm, weights, 1, 1, sems.at[1])
        + half_copies(jac_hbm, jac, 1, 9, sems.at[2])
    )
    pairs = started(half_copies(slot_hbm, slots, 1, 8, sems.at[3]))
    table[...] = jnp.zeros_like(table)
    zero(accs)
    done(nodes)
    table_rows(table, state, 16, 0)
    table_rows(table, ghost_blk, 4, 16)
    table_rows(table, ghost_mer, 2, 20)
    table_rows(table, ghost_ply, 1, 22)
    split_table(table, tparts)
    scatter_rows(conn, rows, 8, 8)
    gather_nodal(conn, tparts, nodal)
    done(points)
    lame, shear, visc = materials_of(ids[...], materials)
    tile = lax.broadcasted_iota(jnp.int32, (8, 128), 0)
    lane = lax.broadcasted_iota(jnp.int32, (8, 128), 1)
    used = jnp.broadcast_to(state[6:7, 0:128], (8, 128)).astype(jnp.int32)
    living = (tile > 0) | (lane + 1024 < used)
    point_stage(jac, weights, nodal, living, lame, shear, visc, grads, pushed, wsg, wpush, wleft, res)
    pair_stage(lame, shear + visc, grads, pushed, wsg, wpush, wleft, blocks, 0)
    done(pairs)
    merge_stage(slots, 8, blocks)
    results = started(
        [
            pltpu.make_async_copy(blocks, blocks_out, sems.at[4, 5]),
            pltpu.make_async_copy(res, res_out, sems.at[4, 6]),
        ]
    )
    mer = (lax.axis_index("mer") < lax.axis_size("mer") - 1).astype(jnp.int32)
    ply = (lax.axis_index("ply") < lax.axis_size("ply") - 1).astype(jnp.int32)
    for n in range(4):
        quads[n] = (12 + n) * 2 + 1
    for n in range(2):
        quads[4 + n] = (10 + n) * 2 + 1
    quads[4 + 2 * mer] = 9 * 2 + 1
    count = 4 + 2 * mer + ply
    run_quads(
        quads, count, (spread0, spread1), (turned0, turned1), accs, rows, index, index_sems,
        slots, blocks, res, 8,
    )
    first = 0
    for n, (part, out) in enumerate([(sum_blk, out_blk), (sum_mer, out_mer), (sum_ply, out_ply)]):
        size = part.shape[0]
        total = accs[0][first : first + size, :]
        for acc in accs[1:]:
            total = total + acc[first : first + size, :]
        part[...] = total
        results += started([pltpu.make_async_copy(part, out, sems.at[4, 9 + n])])
        first += size
    done(results)


def own_kernel(
    materials_hbm, ids_hbm, state_hbm, load_hbm,
    conn_hbm, slot_hbm, jac_hbm, weight_hbm, blocks_hbm, res_hbm,
    residual_out, tangent_out,
    materials, ids, state, load, residual, tangent,
    conn, slots, jac, weights, nodal, table, tparts, grads, pushed, wsg, wpush, wleft,
    spread0, spread1, turned0, turned1, rows, blocks, res, quads, sems, index_sems, *more,
):
    index, accs = more[: AHEAD + 1], more[AHEAD + 1 :]
    nodes = started(
        [pltpu.make_async_copy(state_hbm, state, sems.at[4, 0])]
        + [pltpu.make_async_copy(conn_hbm, conn, sems.at[0, 0])]
    )
    points = started(
        [
            pltpu.make_async_copy(ids_hbm.at[pl.ds(0, 8), :], ids, sems.at[4, 1]),
            pltpu.make_async_copy(materials_hbm, materials, sems.at[4, 13]),
        ]
        + half_copies(weight_hbm, weights, 0, 1, sems.at[1])
        + half_copies(jac_hbm, jac, 0, 9, sems.at[2])
    )
    pairs = started([pltpu.make_async_copy(slot_hbm, slots, sems.at[3, 0])])
    units = started(
        [
            pltpu.make_async_copy(blocks_hbm, blocks.at[pl.ds(VROWS, VROWS), :], sems.at[4, 2]),
            pltpu.make_async_copy(res_hbm, res.at[pl.ds(192, 192), :], sems.at[4, 3]),
            pltpu.make_async_copy(load_hbm, load, sems.at[4, 4]),
        ]
    )
    table[...] = jnp.zeros_like(table)
    zero(accs)
    done(nodes)
    table_rows(table, state, 16, 0)
    split_table(table, tparts)
    scatter_rows(conn, rows, 16, 0)
    gather_nodal(conn, tparts, nodal)
    done(points)
    lame, shear, visc = materials_of(ids[...], materials)
    tile = lax.broadcasted_iota(jnp.int32, (8, 128), 0)
    lane = lax.broadcasted_iota(jnp.int32, (8, 128), 1)
    used = jnp.broadcast_to(state[6:7, 0:128], (8, 128)).astype(jnp.int32)
    living = tile * 128 + lane < used
    point_stage(
        jac, weights, nodal, living, lame, shear, visc, grads, pushed, wsg, wpush, wleft,
        res.at[pl.ds(0, 192), :],
    )
    pair_stage(lame, shear + visc, grads, pushed, wsg, wpush, wleft, blocks, 0)
    done(pairs)
    merge_stage(slots, 16, blocks)
    done(units)

    def put(tile, halves, count):
        for n, half in enumerate(halves):
            quads[count + n] = tile * 2 + half
        return count + len(halves)

    has_mer = lax.axis_index("mer") < lax.axis_size("mer") - 1
    has_ply = lax.axis_index("ply") < lax.axis_size("ply") - 1
    count = 0
    for tile in range(9, 16):
        count = put(tile, (0,), count)
    count = lax.fori_loop(0, (state[6, 0].astype(jnp.int32) + 127) // 128, lambda tile, n: put(tile, (0, 1), n), count)
    count = lax.fori_loop(9, jnp.where(has_ply, 9, 10), lambda tile, n: put(tile, (1,), n), count)
    count = lax.fori_loop(10, jnp.where(has_mer, 10, 12), lambda tile, n: put(tile, (1,), n), count)
    run_quads(
        quads, count, (spread0, spread1), (turned0, turned1), accs, rows, index, index_sems,
        slots, blocks, res, 0,
    )

    def add_up(part):
        total = accs[0][part, :]
        for acc in accs[1:]:
            total = total + acc[part, :]
        return total

    results = []

    def finish(step, carry):
        for k in range(2):
            n = step * 2 + k
            columns = pl.ds(pl.multiple_of(n * 128, 128), 128)
            tangent[0:128, columns] = add_up(pl.ds(n * 256, 128, stride=2)).T
            total = add_up(pl.ds(n * 256 + 1, 128, stride=2)).T
            tangent[128:243, columns] = total[0:115]
            residual[:, columns] = total[115:118] - load[:, columns]
        return carry

    for part in range(4):
        lax.fori_loop(part * 2, part * 2 + 2, finish, 0)
        columns = pl.ds(part * 512, 512)
        results += started(
            [
                pltpu.make_async_copy(tangent.at[:, columns], tangent_out.at[:, columns], sems.at[4, 5 + part]),
                pltpu.make_async_copy(residual.at[:, columns], residual_out.at[:, columns], sems.at[4, 9 + part]),
            ]
        )
    done(results)


def back_kernel(
    residual_in, tangent_in, blk_hbm, mer_hbm, ply_hbm, residual_out, tangent_out,
    blk, mer, ply, residual, tangent, sems,
):
    columns = pl.ds(0, 512)
    done(
        started(
            [
                pltpu.make_async_copy(src, dst, sems.at[n])
                for n, (src, dst) in enumerate(
                    [
                        (blk_hbm, blk),
                        (mer_hbm, mer),
                        (ply_hbm, ply),
                        (residual_in.at[:, columns], residual),
                        (tangent_in.at[:, columns], tangent),
                    ]
                )
            ]
        )
    )
    results = []
    for n in range(4):
        place = pl.ds(n * 128, 128)
        for half in range(2):
            part = pl.ds(n * 256 + half, 128, stride=2)
            total = blk[part, :]
            if n < 2:
                total = total + mer[part, :]
            if n < 1:
                total = total + ply[part, :]
            total = total.T
            if half == 0:
                tangent[0:128, place] += total
            else:
                tangent[128:243, place] += total[0:115]
                residual[:, place] += total[115:118]
        results += started(
            [pltpu.make_async_copy(tangent.at[:, place], tangent_out.at[:, place], sems.at[5 + n])]
        )
    results += started([pltpu.make_async_copy(residual, residual_out.at[:, columns], sems.at[9])])
    done(results)


def scratch_of(table_size, slot_tiles, groups, acc_rows):
    f32, i32 = jnp.float32, jnp.int32
    return (
        [
            pltpu.VMEM((slot_tiles * 8, 128), i32),
            pltpu.VMEM((slot_tiles * 64, 128), i32),
            pltpu.VMEM((8 * 72, 128), f32),
            pltpu.VMEM((64, 128), f32),
            pltpu.VMEM((512, 128), f32),
            pltpu.VMEM((table_size, 128), f32),
            pltpu.VMEM((table_size, 384), jnp.bfloat16),
        ]
        + [pltpu.VMEM((8 * 24 * 8, 128), f32)] * 4
        + [pltpu.VMEM((8 * 6 * 8, 128), f32)]
        + [pltpu.VMEM((256, 128), f32)] * 4
        + [
            pltpu.VMEM((2 * TILES, 4, 128), i32),
            pltpu.VMEM((groups * VROWS, 128), f32),
            pltpu.VMEM((groups * 192, 128), f32),
            pltpu.SMEM((40,), i32),
            pltpu.SemaphoreType.DMA((5, 16)),
            pltpu.SemaphoreType.DMA((AHEAD + 1,)),
        ]
        + [pltpu.SMEM((4, 128), i32)] * (AHEAD + 1)
        + [pltpu.VMEM((acc_rows, 128), f32)] * WAYS
    )


def body(
    connectivity,
    slot_map,
    material_ids,
    element_counts,
    inverse_jacobians,
    quadrature_weights,
    materials,
    displacement,
    previous,
    load,
):
    f32, i32 = jnp.float32, jnp.int32
    count = jnp.broadcast_to(element_counts.astype(f32)[:, None], (1, NODES))
    state = lax.optimization_barrier(jnp.concatenate([displacement, previous, count], axis=0))
    shared = state[:6, :512]
    ghost_blk = shifted(shared, "blk", -1)
    ghost_mer = shifted(shared, "mer", -1)
    ghost_ply = shifted(shared, "ply", -1)
    ids = material_ids.reshape(TILES, 128)
    connectivity, slot_map = tiles_first(connectivity), tiles_first(slot_map)
    inverse_jacobians, quadrature_weights = tiles_first(inverse_jacobians), tiles_first(quadrature_weights)
    anywhere = pl.BlockSpec(memory_space=pl.ANY)
    hbm = pl.BlockSpec(memory_space=pltpu.HBM)
    blocks, res, face_blk, face_mer, face_ply = pl.pallas_call(
        face_kernel,
        out_shape=[
            jax.ShapeDtypeStruct((VROWS, 128), f32),
            jax.ShapeDtypeStruct((192, 128), f32),
            jax.ShapeDtypeStruct((1024, 128), f32),
            jax.ShapeDtypeStruct((512, 128), f32),
            jax.ShapeDtypeStruct((256, 128), f32),
        ],
        in_specs=[hbm] * 3 + [anywhere] * 3 + [hbm] * 4,
        out_specs=[hbm] * 5,
        scratch_shapes=[
            pltpu.SMEM(materials.shape, f32),
            pltpu.VMEM((8, 128), i32),
            pltpu.VMEM((7, NODES), f32),
        ]
        + [pltpu.VMEM((6, 512), f32)] * 3
        + [pltpu.VMEM((rows, 128), f32) for rows in (1024, 512, 256)]
        + scratch_of(192, 8, 1, 1792),
        compiler_params=pltpu.CompilerParams(vmem_limit_bytes=VMEM),
        name="faces",
    )(
        materials, ids, state, ghost_blk, ghost_mer, ghost_ply,
        connectivity, slot_map, inverse_jacobians, quadrature_weights,
    )
    back_ply = shifted(face_ply, "ply", 1)
    back_mer = shifted(face_mer, "mer", 1)
    back_blk = shifted(face_blk, "blk", 1)
    residual, tangent = pl.pallas_call(
        own_kernel,
        out_shape=[
            jax.ShapeDtypeStruct((3, NODES), f32),
            jax.ShapeDtypeStruct((9 * SLOTS, NODES), f32),
        ],
        in_specs=[hbm] * 10,
        out_specs=[hbm] * 2,
        scratch_shapes=[
            pltpu.SMEM(materials.shape, f32),
            pltpu.VMEM((8, 128), i32),
            pltpu.VMEM((7, NODES), f32),
            pltpu.VMEM((3, NODES), f32),
            pltpu.VMEM((3, NODES), f32),
            pltpu.VMEM((9 * SLOTS, NODES), f32),
        ]
        + scratch_of(128, 16, 2, 2 * NODES),
        compiler_params=pltpu.CompilerParams(vmem_limit_bytes=VMEM),
        cost_estimate=pl.CostEstimate(flops=10**8, bytes_accessed=10**8, transcendentals=0),
        name="own",
    )(
        materials, ids, state, load,
        connectivity, slot_map, inverse_jacobians, quadrature_weights, blocks, res,
    )
    return pl.pallas_call(
        back_kernel,
        out_shape=[
            jax.ShapeDtypeStruct((3, NODES), f32),
            jax.ShapeDtypeStruct((9 * SLOTS, NODES), f32),
        ],
        in_specs=[hbm] * 2 + [anywhere] * 3,
        out_specs=[hbm] * 2,
        scratch_shapes=[
            pltpu.VMEM((1024, 128), f32),
            pltpu.VMEM((512, 128), f32),
            pltpu.VMEM((256, 128), f32),
            pltpu.VMEM((3, 512), f32),
            pltpu.VMEM((9 * SLOTS, 512), f32),
            pltpu.SemaphoreType.DMA((10,)),
        ],
        input_output_aliases={0: 0, 1: 1},
        compiler_params=pltpu.CompilerParams(vmem_limit_bytes=8 * 1024 * 1024),
        name="back",
    )(residual, tangent, back_blk, back_mer, back_ply)


def solution(mesh):
    return jax.shard_map(
        body,
        mesh=mesh,
        in_specs=(
            P(None, ("blk", "mer", "ply")),
            P(None, ("blk", "mer", "ply")),
            P(("blk", "mer", "ply")),
            P(("blk", "mer", "ply")),
            P(None, ("blk", "mer", "ply")),
            P(None, ("blk", "mer", "ply")),
            P(),
            P(None, ("blk", "mer", "ply")),
            P(None, ("blk", "mer", "ply")),
            P(None, ("blk", "mer", "ply")),
        ),
        out_specs=(P(None, ("blk", "mer", "ply")), P(None, ("blk", "mer", "ply"))),
        check_vma=False,
    )
```
